512 devices in a mesh: dp: 4 (over x), ctx: 32 (over y_lo, z), tp: 4 (over y_hi, core).
Axes of the slice: x: 4, y: 8 (y_hi: 2, y_lo: 4; y = y_hi * 4 + y_lo), z: 8, core: 2. Of those that a mesh axis runs over, the one named last changes fastest.
Arguments:
- queries: bfloat16 [4, 4096, 4096], P('dp', 'ctx', 'tp'), may hold values from -156 to 156
- keys: bfloat16 [4, 4096, 512], P('dp', 'ctx', 'tp'), may hold values from -6 to 6
- values: bfloat16 [4, 4096, 512], P('dp', 'ctx', 'tp'), may hold values from -6 to 6
- out_grad: bfloat16 [4, 4096, 4096], P('dp', 'ctx', 'tp'), may hold values from -6 to 6
- normed_input: bfloat16 [4, 4096, 8192], P('dp', 'ctx', 'tp'), may hold values from -6 to 6
- doc_lengths: int32 [4, 8], P('dp'), may hold values from 1 to 2048, 4096 in all within a row
- span_order: int32 [32], replicated, may hold values from 0 to 31, each once
Outputs:
- query_grad: bfloat16 [4, 4096, 4096], P('dp', 'ctx', 'tp')
- key_grad: bfloat16 [4, 4096, 512], P('dp', 'ctx', 'tp')
- value_grad: bfloat16 [4, 4096, 512], P('dp', 'ctx', 'tp')
- key_weight_grad: float32 [8192, 512], P('ctx', 'tp')
- value_weight_grad: float32 [8192, 512], P('ctx', 'tp')
The draws below stay inside these ranges and needn't reach their ends.
Inputs may be any that keep to these rules, and one draw needn't show every extreme that they name: `doc_lengths`: each row sums to 4096; the longest document of each row has exactly 2048 positions. `span_order`: each value once.
All inputs are finite; a program needn't handle non-finite values.
Results may differ from the reference program's by a relative error of at most 0.0095.
Values may be sent and summed in bfloat16 or wider, within the bound.
No kernel may reach another device: no remote copies, remote signals or barrier semaphores. Data moves between devices by JAX's collectives and lax.ppermute only.
A program may use at most 64 MiB of HBM per device.

```python
import math
import jax
import jax.numpy as jnp
import numpy as np
from jax import lax

MODEL_WIDTH = 8192
QUERY_HEADS = 32
KEY_VALUE_HEADS = 4
HEAD_WIDTH = 128
SPAN = 64
DOCS = 8
BATCH_SEQUENCES = 4
WINDOW_LENGTH = 4096
N_CTX = 32


def shared_keys(key):
    return jnp.clip(jax.random.normal(key, (BATCH_SEQUENCES, WINDOW_LENGTH, KEY_VALUE_HEADS * HEAD_WIDTH), jnp.float32), -6.0, 6.0)


def draw_keys(key, part):
    base_offset = shared_keys(key)
    return base_offset.astype(jnp.bfloat16)


def draw_queries(key, part):
    key = jax.random.fold_in(key, 7)
    fresh = jnp.clip(jax.random.normal(key, (BATCH_SEQUENCES, WINDOW_LENGTH, QUERY_HEADS * HEAD_WIDTH), jnp.float32), -6.0, 6.0)
    return fresh.astype(jnp.bfloat16)


def block_levels(own_key, dims, cuts, least, high):
    def one(dim, parts):
        steps = jax.random.uniform(jax.random.fold_in(jax.random.fold_in(own_key, 6), dim), (parts,), jnp.float32, least / len(cuts), high / len(cuts))
        return jnp.repeat(jnp.exp(steps), dims[dim] // parts).reshape((-1,) + (1,) * (len(dims) - dim - 1))

    factor_of = one(*cuts[0])
    for cut in cuts[1:]:
        factor_of = factor_of * one(*cut)
    return factor_of


def split_up(number_of, total, most, lean):
    portions = [(1 << 20) // math.isqrt(grade ** lean) + 1 for grade in range(2, number_of + 1)]
    rest, holding = total - most - (number_of - 1), [1] * (number_of - 1)
    while rest > 0:
        movable = [i for i in range(number_of - 1) if holding[i] < most]
        pool, left = sum([portions[i] for i in movable]), rest
        for i in movable:
            addition = min(most - holding[i], max(1, left * portions[i] // pool), rest)
            holding[i] = holding[i] + addition
            rest = rest - addition
    return np.array([most] + holding)


def uneven_parts(key, amount, total, most, slope):
    if amount == 2:
        one = jax.random.randint(key, (), max(1, total - most), min(most, total - 1) + 1)
        return jnp.stack([one, total - one])
    sizes = jnp.asarray(split_up(amount, total, most, slope), jnp.int32)
    couples = (amount - 1) // 2
    source_of, receiver = sizes[1:1 + 2 * couples:2], sizes[2:2 + 2 * couples:2]
    room = jnp.minimum(source_of - 1, most - receiver)
    passed = jax.random.randint(jax.random.fold_in(key, 1), (couples,), 0, 1 << 20) % (room + 1)
    sizes = sizes.at[1:1 + 2 * couples:2].set(source_of - passed).at[2:2 + 2 * couples:2].set(receiver + passed)
    return sizes[jax.random.permutation(jax.random.fold_in(key, 2), amount)]


def centred(rng, shape, scale, limit, split=(), kind=jnp.bfloat16):
    values = scale * jax.random.normal(rng, shape, jnp.float32)
    if split:
        values = values * block_levels(rng, shape, split, -0.22, 0.18)
    return jnp.clip(values, -limit, limit).astype(kind)


def setup_inputs(seed: int = 0) -> dict:
    splits = jax.random.split(jax.random.key(seed), 8)
    queries = draw_queries(jax.random.fold_in(splits[7], 71), 0)
    keys = draw_keys(jax.random.fold_in(splits[7], 71), 0)
    values = centred(splits[2], (BATCH_SEQUENCES, WINDOW_LENGTH, KEY_VALUE_HEADS * HEAD_WIDTH), 1.0, 6.0, ((0, 4), (1, 32), (2, 4)))
    out_grad = centred(splits[3], (BATCH_SEQUENCES, WINDOW_LENGTH, QUERY_HEADS * HEAD_WIDTH), 1.0, 6.0, ((0, 4), (1, 32), (2, 4)))
    normed_input = centred(splits[4], (BATCH_SEQUENCES, WINDOW_LENGTH, MODEL_WIDTH), 1.0, 6.0, ((0, 4), (1, 32), (2, 4)))
    doc_lengths = jax.vmap(lambda own: uneven_parts(own, DOCS, WINDOW_LENGTH, WINDOW_LENGTH // 2, 2))(jax.random.split(splits[5], BATCH_SEQUENCES)).reshape((BATCH_SEQUENCES, DOCS)).astype(jnp.int32)
    span_order = jax.random.permutation(splits[6], N_CTX).astype(jnp.int32)
    return dict(queries=queries, keys=keys, values=values, out_grad=out_grad, normed_input=normed_input, doc_lengths=doc_lengths, span_order=span_order)


def stored_positions(span_order):
    stored = jnp.arange(WINDOW_LENGTH, dtype=jnp.int32)
    owner = stored // (2 * SPAN)
    within = stored % (2 * SPAN)
    first = span_order[owner]
    blocks = jnp.where(within < SPAN, first, 2 * N_CTX - 1 - first)
    return (blocks * SPAN + within % SPAN).astype(jnp.int32)


def document_ids(positions, lengths):
    boundary = jnp.cumsum(lengths)
    return jnp.sum((boundary[None, :] <= positions[:, None]).astype(jnp.int32), axis=1)


def attention_head(query_block, grad_block, key_block, value_block, allowed):
    factor = HEAD_WIDTH ** -0.5
    scores = jnp.dot(query_block, key_block.T, preferred_element_type=jnp.float32) * factor
    masked = jnp.where(allowed, scores, -1e30)
    row_max = jnp.max(masked, axis=1, keepdims=True)
    summed = jnp.sum(jnp.where(allowed, jnp.exp(masked - row_max), 0.0), axis=1, keepdims=True)
    log_norm = row_max + jnp.log(summed)
    probabilities = jnp.where(allowed, jnp.exp(scores - log_norm), 0.0)
    prob_grad = jnp.dot(grad_block, value_block.T, preferred_element_type=jnp.float32)
    row_drift = jnp.sum(probabilities * prob_grad, axis=1, keepdims=True)
    score_grad = (probabilities * (prob_grad - row_drift)).astype(jnp.bfloat16)
    query_part = jnp.dot(score_grad, key_block, preferred_element_type=jnp.float32) * factor
    key_part = jnp.dot(score_grad.T, query_block, preferred_element_type=jnp.float32) * factor
    value_part = jnp.dot(probabilities.astype(jnp.bfloat16).T, grad_block, preferred_element_type=jnp.float32)
    return query_part, key_part, value_part


def reference(queries, keys, values, out_grad, normed_input, doc_lengths, span_order):
    group_size = QUERY_HEADS // KEY_VALUE_HEADS
    positions = stored_positions(span_order)
    causal = positions[None, :] <= positions[:, None]
    query_list, key_list, value_list = [], [], []
    key_matrix = jnp.zeros((MODEL_WIDTH, KEY_VALUE_HEADS * HEAD_WIDTH), jnp.float32)
    value_matrix = jnp.zeros((MODEL_WIDTH, KEY_VALUE_HEADS * HEAD_WIDTH), jnp.float32)
    for batch_row in range(BATCH_SEQUENCES):
        documents = document_ids(positions, doc_lengths[batch_row])
        allowed = causal & (documents[None, :] == documents[:, None])
        query_parts, key_parts, value_parts = [], [], []
        for key_value_head in range(KEY_VALUE_HEADS):
            key_block = keys[batch_row, :, key_value_head * HEAD_WIDTH:(key_value_head + 1) * HEAD_WIDTH]
            value_block = values[batch_row, :, key_value_head * HEAD_WIDTH:(key_value_head + 1) * HEAD_WIDTH]
            lower = key_value_head * group_size * HEAD_WIDTH
            upper = (key_value_head + 1) * group_size * HEAD_WIDTH
            head_queries = queries[batch_row, :, lower:upper].reshape(WINDOW_LENGTH, group_size, HEAD_WIDTH).transpose(1, 0, 2)
            head_grads = out_grad[batch_row, :, lower:upper].reshape(WINDOW_LENGTH, group_size, HEAD_WIDTH).transpose(1, 0, 2)

            def head_step(carry, pieces, key_block=key_block, value_block=value_block, allowed=allowed):
                query_part, key_part, value_part = attention_head(pieces[0], pieces[1], key_block, value_block, allowed)
                return (carry[0] + key_part, carry[1] + value_part), query_part

            empty = jnp.zeros((WINDOW_LENGTH, HEAD_WIDTH), jnp.float32)
            sums, query_heads = lax.scan(head_step, (empty, empty), (head_queries, head_grads))
            query_parts.append(query_heads.transpose(1, 0, 2).reshape(WINDOW_LENGTH, group_size * HEAD_WIDTH))
            key_parts.append(sums[0])
            value_parts.append(sums[1])
        query_list.append(jnp.concatenate(query_parts, axis=1).astype(jnp.bfloat16))
        key_rounded = jnp.concatenate(key_parts, axis=1).astype(jnp.bfloat16)
        value_rounded = jnp.concatenate(value_parts, axis=1).astype(jnp.bfloat16)
        key_list.append(key_rounded)
        value_list.append(value_rounded)
        key_matrix = key_matrix + jnp.dot(normed_input[batch_row].T, key_rounded, preferred_element_type=jnp.float32)
        value_matrix = value_matrix + jnp.dot(normed_input[batch_row].T, value_rounded, preferred_element_type=jnp.float32)
    return (jnp.stack(query_list), jnp.stack(key_list), jnp.stack(value_list), key_matrix, value_matrix)
```

```python
import functools

import jax
import jax.numpy as jnp
from jax import lax
from jax.experimental import pallas as pl
from jax.experimental.pallas import tpu as pltpu
from jax.sharding import Mesh, PartitionSpec as P

HEAD = 128
SPAN = 64
TILE = 256
SPANS_PER_TILE = TILE // SPAN
NEG = -1e30
SCALE = HEAD ** (-0.5)
VMEM_LIMIT = 40 * 1024 * 1024


def nt(left, right):
    return lax.dot_general(left, right, (((1,), (1,)), ((), ())), preferred_element_type=jnp.float32)


def nn(left, right):
    return lax.dot_general(left, right, (((1,), (0,)), ((), ())), preferred_element_type=jnp.float32)


def load_operands(meta, own, other, kv, q_s, g_s, k_s, v_s, pos_s):
    heads = own.shape[2] // HEAD
    rows = heads * SPAN
    for source, block in enumerate((own, other)):
        for half in range(2):
            base = (source * 2 + half) * rows
            for head in range(heads):
                here = pl.ds(base + head * SPAN, SPAN)
                q_s[here, :] = block[0, half * SPAN:(half + 1) * SPAN, head * HEAD:(head + 1) * HEAD]
                g_s[here, :] = block[1, half * SPAN:(half + 1) * SPAN, head * HEAD:(head + 1) * HEAD]
    lane_rows = lax.broadcasted_iota(jnp.int32, (SPAN, 128), 0)

    def place(block, carry):
        for half in range(2):
            span = 2 * block + half
            start = pl.multiple_of(meta[0, span] * SPAN, SPAN)
            piece = kv[block, half * SPAN:(half + 1) * SPAN, :]
            k_s[pl.ds(start, SPAN), :] = piece[:, :HEAD]
            v_s[pl.ds(start, SPAN), :] = piece[:, HEAD:]
            pos_s[pl.ds(start, SPAN), :] = lane_rows + meta[1, span] * SPAN
        return carry

    lax.fori_loop(0, kv.shape[0], place, 0)


def masked_scores(k_tile, q_rows, pos_tile, q_pos, q_start):
    copies = q_rows.shape[0] // 128
    key_pos = jnp.concatenate([pos_tile] * copies, axis=1)
    mask = (key_pos <= q_pos) & (key_pos >= q_start)
    return jnp.where(mask, nt(k_tile, q_rows) * SCALE, NEG)


def stats_kernel(meta, qmeta, own, other, kv, out, q_s, g_s, k_s, v_s, pos_s):
    load_operands(meta, own, other, kv, q_s, g_s, k_s, v_s, pos_s)
    rows = q_s.shape[0] // 4

    def span_step(u, carry):
        q_rows = q_s[pl.ds(u * rows, rows), :]
        g_rows = g_s[pl.ds(u * rows, rows), :]
        q_pos = qmeta[pl.ds(u, 1), :]
        q_start = qmeta[pl.ds(4 + u, 1), :]

        def tile_step(t, state):
            top, total, weighted = state
            here = pl.ds(pl.multiple_of(t * TILE, TILE), TILE)
            scores = masked_scores(k_s[here, :], q_rows, pos_s[here, :], q_pos, q_start)
            new_top = jnp.maximum(top, jnp.max(scores, axis=0, keepdims=True))
            probs = jnp.exp(scores - new_top)
            keep = jnp.exp(top - new_top)
            grad = nt(v_s[here, :], g_rows)
            return (
                new_top,
                keep * total + jnp.sum(probs, axis=0, keepdims=True),
                keep * weighted + jnp.sum(probs * grad, axis=0, keepdims=True),
            )

        zero = jnp.zeros((1, rows), jnp.float32)
        top, total, weighted = lax.fori_loop(
            meta[2, u], meta[2, 4 + u], tile_step, (jnp.full((1, rows), NEG, jnp.float32), zero, zero)
        )
        out[pl.ds(u, 1), :] = top
        out[pl.ds(4 + u, 1), :] = total
        out[pl.ds(8 + u, 1), :] = weighted
        return carry

    lax.fori_loop(0, 4, span_step, 0)
    out[12:16, :] = jnp.zeros((4, rows), jnp.float32)


def grad_kernel(
    meta, qmeta, own, other, kv, stats, far, dq_own, dq_other, dkv,
    q_s, g_s, k_s, v_s, pos_s, kt_s, dk_s, dv_s, dq_s, fin_s,
):
    load_operands(meta, own, other, kv, q_s, g_s, k_s, v_s, pos_s)
    rows = q_s.shape[0] // 4
    heads = rows // SPAN
    tiles = k_s.shape[0] // TILE
    for t in range(tiles):
        kt_s[t] = k_s[t * TILE:(t + 1) * TILE, :].T
    dk_s[...] = jnp.zeros_like(dk_s)
    dv_s[...] = jnp.zeros_like(dv_s)
    for u in range(4):
        v = (u + 2) % 4
        top_a, top_b = stats[u:u + 1, :], far[v:v + 1, :]
        top = jnp.maximum(top_a, top_b)
        scale_a, scale_b = jnp.exp(top_a - top), jnp.exp(top_b - top)
        total = scale_a * stats[4 + u:5 + u, :] + scale_b * far[4 + v:5 + v, :]
        weighted = scale_a * stats[8 + u:9 + u, :] + scale_b * far[8 + v:9 + v, :]
        fin_s[u:u + 1, :] = top + jnp.log(total)
        fin_s[4 + u:5 + u, :] = weighted / total

    def span_step(u, carry):
        q_rows = q_s[pl.ds(u * rows, rows), :]
        g_rows = g_s[pl.ds(u * rows, rows), :]
        q_pos = qmeta[pl.ds(u, 1), :]
        q_start = qmeta[pl.ds(4 + u, 1), :]
        log_norm = fin_s[pl.ds(u, 1), :]
        drift = fin_s[pl.ds(4 + u, 1), :]
        dq_s[...] = jnp.zeros_like(dq_s)

        def tile_step(t, inner):
            here = pl.ds(pl.multiple_of(t * TILE, TILE), TILE)
            scores = masked_scores(k_s[here, :], q_rows, pos_s[here, :], q_pos, q_start)
            probs = jnp.exp(scores - log_norm)
            grad = nt(v_s[here, :], g_rows)
            score_grad = (probs * (grad - drift)).astype(jnp.bfloat16)
            dv_s[here, :] += nn(probs.astype(jnp.bfloat16), g_rows)
            dk_s[here, :] += nn(score_grad, q_rows)
            dq_s[...] += nn(kt_s[t], score_grad)
            return inner

        lax.fori_loop(meta[2, u], meta[2, 4 + u], tile_step, 0)
        flat = (dq_s[...] * SCALE).T
        half = pl.multiple_of(lax.rem(u, 2) * SPAN, SPAN)

        @pl.when(u < 2)
        def _():
            for head in range(heads):
                dq_own[pl.ds(half, SPAN), head * HEAD:(head + 1) * HEAD] = flat[head * SPAN:(head + 1) * SPAN, :]

        @pl.when(u >= 2)
        def _():
            for head in range(heads):
                dq_other[pl.ds(half, SPAN), head * HEAD:(head + 1) * HEAD] = flat[
                    head * SPAN:(head + 1) * SPAN, :
                ].astype(jnp.bfloat16)

        return carry

    lax.fori_loop(0, 4, span_step, 0)

    def unplace(block, carry):
        for half in range(2):
            start = pl.multiple_of(meta[0, 2 * block + half] * SPAN, SPAN)
            here = pl.ds(start, SPAN)
            dkv[block, half * SPAN:(half + 1) * SPAN, :HEAD] = (dk_s[here, :] * SCALE).astype(jnp.bfloat16)
            dkv[block, half * SPAN:(half + 1) * SPAN, HEAD:] = dv_s[here, :].astype(jnp.bfloat16)
        return carry

    lax.fori_loop(0, dkv.shape[0], unplace, 0)


def operand_scratch(rows, keys):
    return [
        pltpu.VMEM((4 * rows, HEAD), jnp.bfloat16),
        pltpu.VMEM((4 * rows, HEAD), jnp.bfloat16),
        pltpu.VMEM((keys, HEAD), jnp.bfloat16),
        pltpu.VMEM((keys, HEAD), jnp.bfloat16),
        pltpu.VMEM((keys, 128), jnp.int32),
    ]


def in_vmem(count):
    return [pl.BlockSpec(memory_space=pltpu.SMEM)] + [pl.BlockSpec(memory_space=pltpu.VMEM)] * count


def stats_call(meta, qmeta, own, other, kv):
    rows = own.shape[2] // HEAD * SPAN
    keys = kv.shape[0] * kv.shape[1]
    return pl.pallas_call(
        stats_kernel,
        out_shape=jax.ShapeDtypeStruct((16, rows), jnp.float32),
        in_specs=in_vmem(4),
        out_specs=pl.BlockSpec(memory_space=pltpu.VMEM),
        scratch_shapes=operand_scratch(rows, keys),
        compiler_params=pltpu.CompilerParams(vmem_limit_bytes=VMEM_LIMIT),
        cost_estimate=pl.CostEstimate(flops=2 * 10**9, bytes_accessed=4 * 10**6, transcendentals=10**6),
        name="stats",
    )(meta, qmeta, own, other, kv)


def grad_call(meta, qmeta, own, other, kv, stats, far):
    rows = own.shape[2] // HEAD * SPAN
    keys = kv.shape[0] * kv.shape[1]
    height, width = own.shape[1:]
    return pl.pallas_call(
        grad_kernel,
        out_shape=(
            jax.ShapeDtypeStruct((height, width), jnp.float32),
            jax.ShapeDtypeStruct((height, width), jnp.bfloat16),
            jax.ShapeDtypeStruct(kv.shape, jnp.bfloat16),
        ),
        in_specs=in_vmem(6),
        out_specs=[pl.BlockSpec(memory_space=pltpu.VMEM)] * 3,
        scratch_shapes=operand_scratch(rows, keys) + [
            pltpu.VMEM((keys // TILE, HEAD, TILE), jnp.bfloat16),
            pltpu.VMEM((keys, HEAD), jnp.float32),
            pltpu.VMEM((keys, HEAD), jnp.float32),
            pltpu.VMEM((HEAD, rows), jnp.float32),
            pltpu.VMEM((8, rows), jnp.float32),
        ],
        compiler_params=pltpu.CompilerParams(vmem_limit_bytes=VMEM_LIMIT),
        cost_estimate=pl.CostEstimate(flops=5 * 10**9, bytes_accessed=6 * 10**6, transcendentals=10**6),
        name="grads",
    )(meta, qmeta, own, other, kv, stats, far)


def swapped(array, axis):
    return lax.ppermute(array, axis, [(0, 1), (1, 0)])


def tables(doc_lengths, span_order):
    count = span_order.shape[0]
    outer, inner = lax.axis_size("ya"), lax.axis_size("z")
    side = lax.axis_index("yb")
    boundary = jnp.cumsum(doc_lengths[0])
    order = span_order.reshape(outer, 2, inner)
    mine = jnp.where(side == 0, order[:, 0], order[:, 1]).reshape(-1)
    spans = jnp.stack([mine, 2 * count - 1 - mine], axis=1).reshape(-1)
    rank = jnp.sum((spans[None, :] < spans[:, None]).astype(jnp.int32), axis=1)
    ctx = lax.axis_index(("ya", "yb", "z"))
    ids = jnp.arange(count, dtype=jnp.int32)
    first = jnp.sum(jnp.where(ids == ctx, span_order, 0))
    partner = ctx + (1 - 2 * side) * inner
    second = jnp.sum(jnp.where(ids == partner, span_order, 0))
    q_spans = jnp.stack([first, 2 * count - 1 - first, second, 2 * count - 1 - second])

    def doc_start(positions):
        reached = boundary <= positions[..., None]
        return jnp.max(jnp.where(reached, boundary, 0), axis=-1)

    low = doc_start(q_spans * SPAN) // SPAN
    lower = jnp.sum((spans[None, :] < low[:, None]).astype(jnp.int32), axis=1) // SPANS_PER_TILE
    upper = jnp.sum((spans[None, :] <= q_spans[:, None]).astype(jnp.int32), axis=1)
    upper = (upper + SPANS_PER_TILE - 1) // SPANS_PER_TILE
    bounds = jnp.concatenate([lower, upper, jnp.zeros((spans.shape[0] - 8,), jnp.int32)])
    meta = jnp.stack([rank, spans, bounds])
    return meta, q_spans, doc_start


def shards(queries, keys, values, out_grad, normed_input, doc_lengths, span_order):
    height = queries.shape[1]
    heads = queries.shape[2] // HEAD
    group = ("ya", "z")
    group_size = lax.axis_size("ya") * lax.axis_size("z")
    depth = lax.axis_size("z")

    own = jnp.concatenate([queries, out_grad], axis=0)
    other = swapped(own, "yb")
    pair = jnp.concatenate([keys[0], values[0]], axis=1)
    kv = lax.all_to_all(
        jnp.broadcast_to(pair[None], (group_size,) + pair.shape), group, 0, 0, tiled=True
    )

    meta, q_spans, doc_start = tables(doc_lengths, span_order)
    q_pos = q_spans[:, None] * SPAN + jnp.arange(SPAN, dtype=jnp.int32)[None, :]
    q_start = doc_start(q_pos)
    qmeta = jnp.tile(jnp.concatenate([q_pos, q_start], axis=0), (1, heads))

    stats = stats_call(meta, qmeta, own, other, kv)
    far = swapped(stats, "yb")

    width = normed_input.shape[2] // depth
    columns = lax.all_to_all(
        normed_input[0].reshape(height, depth, width), "z", split_axis=1, concat_axis=0, tiled=True
    ).reshape(depth * height, width)
    beside = swapped(columns, "yh")
    both = jnp.stack([columns, beside])
    across = swapped(both, "core")

    dq_own, dq_other, dkv = grad_call(meta, qmeta, own, other, kv, stats, far)
    dq_far = swapped(dq_other, "yb")
    parts = lax.all_to_all(dkv, group, 0, 0, tiled=True)
    own_grads = jnp.sum(parts.astype(jnp.float32), axis=0).astype(jnp.bfloat16)
    query_grad = (dq_own + dq_far.astype(jnp.float32)).astype(jnp.bfloat16)[None]

    all_grads = lax.all_to_all(
        jnp.broadcast_to(own_grads[None], (depth,) + own_grads.shape), "z", 0, 0, tiled=True
    ).reshape(depth * height, 2 * HEAD)

    def weights(features):
        return lax.dot_general(
            features, all_grads, (((1,), (0,)), ((), ())), preferred_element_type=jnp.float32
        )

    near = weights(both)
    far_weights = weights(across)
    core, high = lax.axis_index("core"), lax.axis_index("yh")
    by_core = jnp.where(
        core == 0, jnp.stack([near, far_weights], axis=1), jnp.stack([far_weights, near], axis=1)
    )
    by_high = jnp.where(high == 0, by_core, by_core[::-1]).astype(jnp.bfloat16)
    blocks = by_high.reshape((4,) + by_high.shape[2:])
    pieces = lax.all_to_all(blocks, ("ya", "yb"), 0, 0, tiled=True)
    partial = jnp.sum(pieces.astype(jnp.float32), axis=0).astype(jnp.bfloat16)
    spread = lax.all_to_all(
        jnp.broadcast_to(partial[None], (lax.axis_size("dp"),) + partial.shape), "dp", 0, 0, tiled=True
    )
    weight_total = jnp.sum(spread.astype(jnp.float32), axis=0)
    return (
        query_grad,
        own_grads[None, :, :HEAD],
        own_grads[None, :, HEAD:],
        weight_total[:, :HEAD],
        weight_total[:, HEAD:],
    )


def solution(mesh):
    sizes = dict(mesh.shape)
    deep = sizes["ctx"] // 4
    fine = Mesh(
        mesh.devices.reshape(sizes["dp"], 2, 2, deep, 2, sizes["tp"] // 2),
        ("dp", "ya", "yb", "z", "yh", "core"),
    )
    context, model = ("ya", "yb", "z"), ("yh", "core")
    in_specs = (
        P("dp", context, model),
        P("dp", context, model),
        P("dp", context, model),
        P("dp", context, model),
        P("dp", context, model),
        P("dp", None),
        P(),
    )
    out_specs = (
        P("dp", context, model),
        P("dp", context, model),
        P("dp", context, model),
        P(context, model),
        P(context, model),
    )
    return jax.shard_map(shards, mesh=fine, in_specs=in_specs, out_specs=out_specs, check_vma=False)
```

```python
import jax
import jax.numpy as jnp
from jax import lax
from jax.experimental import pallas as pl
from jax.experimental.pallas import tpu as pltpu
from jax.sharding import Mesh, PartitionSpec as P

HEAD = 128
SPAN = 64
TILE = 256
SPANS_PER_TILE = TILE // SPAN
NEG = -1e30
SCALE = HEAD ** (-0.5)
VMEM_LIMIT = 40 * 1024 * 1024


def nt(left, right):
    return lax.dot_general(left, right, (((1,), (1,)), ((), ())), preferred_element_type=jnp.float32)


def nn(left, right):
    return lax.dot_general(left, right, (((1,), (0,)), ((), ())), preferred_element_type=jnp.float32)


def load_operands(meta, own, other, kv, q_s, g_s, k_s, v_s, pos_s):
    heads = own.shape[2] // HEAD
    rows = heads * SPAN
    for source, block in enumerate((own, other)):
        for half in range(2):
            base = (source * 2 + half) * rows
            for head in range(heads):
                here = pl.ds(base + head * SPAN, SPAN)
                q_s[here, :] = block[0, half * SPAN:(half + 1) * SPAN, head * HEAD:(head + 1) * HEAD]
                g_s[here, :] = block[1, half * SPAN:(half + 1) * SPAN, head * HEAD:(head + 1) * HEAD]
    lane_rows = lax.broadcasted_iota(jnp.int32, (SPAN, 128), 0)

    def place(block, carry):
        for half in range(2):
            span = 2 * block + half
            start = pl.multiple_of(meta[0, span] * SPAN, SPAN)
            piece = kv[block, half * SPAN:(half + 1) * SPAN, :]
            k_s[pl.ds(start, SPAN), :] = piece[:, :HEAD]
            v_s[pl.ds(start, SPAN), :] = piece[:, HEAD:]
            pos_s[pl.ds(start, SPAN), :] = lane_rows + meta[1, span] * SPAN
        return carry

    lax.fori_loop(0, kv.shape[0], place, 0)


def masked_scores(k_tile, q_rows, pos_tile, q_pos, q_start):
    copies = q_rows.shape[0] // 128
    key_pos = jnp.concatenate([pos_tile] * copies, axis=1)
    mask = (key_pos <= q_pos) & (key_pos >= q_start)
    return jnp.where(mask, nt(k_tile, q_rows) * SCALE, NEG)


def stats_kernel(meta, qmeta, own, other, kv, out, q_s, g_s, k_s, v_s, pos_s):
    load_operands(meta, own, other, kv, q_s, g_s, k_s, v_s, pos_s)
    rows = q_s.shape[0] // 4

    def span_step(u, carry):
        q_rows = q_s[pl.ds(u * rows, rows), :]
        g_rows = g_s[pl.ds(u * rows, rows), :]
        q_pos = qmeta[pl.ds(u, 1), :]
        q_start = qmeta[pl.ds(4 + u, 1), :]

        def tile_step(t, state):
            top, total, weighted = state
            here = pl.ds(pl.multiple_of(t * TILE, TILE), TILE)
            scores = masked_scores(k_s[here, :], q_rows, pos_s[here, :], q_pos, q_start)
            new_top = jnp.maximum(top, jnp.max(scores, axis=0, keepdims=True))
            probs = jnp.exp(scores - new_top)
            keep = jnp.exp(top - new_top)
            grad = nt(v_s[here, :], g_rows)
            return (
                new_top,
                keep * total + jnp.sum(probs, axis=0, keepdims=True),
                keep * weighted + jnp.sum(probs * grad, axis=0, keepdims=True),
            )

        zero = jnp.zeros((1, rows), jnp.float32)
        top, total, weighted = lax.fori_loop(
            meta[2, u], meta[2, 4 + u], tile_step, (jnp.full((1, rows), NEG, jnp.float32), zero, zero)
        )
        out[pl.ds(u, 1), :] = top
        out[pl.ds(4 + u, 1), :] = total
        out[pl.ds(8 + u, 1), :] = weighted
        return carry

    lax.fori_loop(0, 4, span_step, 0)
    out[12:16, :] = jnp.zeros((4, rows), jnp.float32)


def grad_kernel(
    meta, qmeta, own, other, kv, stats, far, dq_own, dq_other, dkv,
    q_s, g_s, k_s, v_s, pos_s, kt_s, dk_s, dv_s, dq_s, fin_s,
):
    load_operands(meta, own, other, kv, q_s, g_s, k_s, v_s, pos_s)
    rows = q_s.shape[0] // 4
    heads = rows // SPAN
    tiles = k_s.shape[0] // TILE
    for t in range(tiles):
        kt_s[t] = k_s[t * TILE:(t + 1) * TILE, :].T
    dk_s[...] = jnp.zeros_like(dk_s)
    dv_s[...] = jnp.zeros_like(dv_s)
    for u in range(4):
        v = (u + 2) % 4
        top_a, top_b = stats[u:u + 1, :], far[v:v + 1, :]
        top = jnp.maximum(top_a, top_b)
        scale_a, scale_b = jnp.exp(top_a - top), jnp.exp(top_b - top)
        total = scale_a * stats[4 + u:5 + u, :] + scale_b * far[4 + v:5 + v, :]
        weighted = scale_a * stats[8 + u:9 + u, :] + scale_b * far[8 + v:9 + v, :]
        fin_s[u:u + 1, :] = top + jnp.log(total)
        fin_s[4 + u:5 + u, :] = weighted / total

    def span_step(u, carry):
        q_rows = q_s[pl.ds(u * rows, rows), :]
        g_rows = g_s[pl.ds(u * rows, rows), :]
        q_pos = qmeta[pl.ds(u, 1), :]
        q_start = qmeta[pl.ds(4 + u, 1), :]
        log_norm = fin_s[pl.ds(u, 1), :]
        drift = fin_s[pl.ds(4 + u, 1), :]
        dq_s[...] = jnp.zeros_like(dq_s)

        def tile_step(t, inner):
            here = pl.ds(pl.multiple_of(t * TILE, TILE), TILE)
            scores = masked_scores(k_s[here, :], q_rows, pos_s[here, :], q_pos, q_start)
            probs = jnp.exp(scores - log_norm)
            grad = nt(v_s[here, :], g_rows)
            score_grad = (probs * (grad - drift)).astype(jnp.bfloat16)
            dv_s[here, :] += nn(probs.astype(jnp.bfloat16), g_rows)
            dk_s[here, :] += nn(score_grad, q_rows)
            dq_s[...] += nn(kt_s[t], score_grad)
            return inner

        lax.fori_loop(meta[2, u], meta[2, 4 + u], tile_step, 0)
        flat = (dq_s[...] * SCALE).T
        half = pl.multiple_of(lax.rem(u, 2) * SPAN, SPAN)

        @pl.when(u < 2)
        def _():
            for head in range(heads):
                dq_own[pl.ds(half, SPAN), head * HEAD:(head + 1) * HEAD] = flat[head * SPAN:(head + 1) * SPAN, :]

        @pl.when(u >= 2)
        def _():
            for head in range(heads):
                dq_other[pl.ds(half, SPAN), head * HEAD:(head + 1) * HEAD] = flat[
                    head * SPAN:(head + 1) * SPAN, :
                ].astype(jnp.bfloat16)

        return carry

    lax.fori_loop(0, 4, span_step, 0)

    def unplace(block, carry):
        for half in range(2):
            start = pl.multiple_of(meta[0, 2 * block + half] * SPAN, SPAN)
            here = pl.ds(start, SPAN)
            dkv[block, half * SPAN:(half + 1) * SPAN, :HEAD] = (dk_s[here, :] * SCALE).astype(jnp.bfloat16)
            dkv[block, half * SPAN:(half + 1) * SPAN, HEAD:] = dv_s[here, :].astype(jnp.bfloat16)
        return carry

    lax.fori_loop(0, dkv.shape[0], unplace, 0)


def operand_scratch(rows, keys):
    return [
        pltpu.VMEM((4 * rows, HEAD), jnp.bfloat16),
        pltpu.VMEM((4 * rows, HEAD), jnp.bfloat16),
        pltpu.VMEM((keys, HEAD), jnp.bfloat16),
        pltpu.VMEM((keys, HEAD), jnp.bfloat16),
        pltpu.VMEM((keys, 128), jnp.int32),
    ]


def in_vmem(count):
    return [pl.BlockSpec(memory_space=pltpu.SMEM)] + [pl.BlockSpec(memory_space=pltpu.VMEM)] * count


def stats_call(meta, qmeta, own, other, kv):
    rows = own.shape[2] // HEAD * SPAN
    keys = kv.shape[0] * kv.shape[1]
    return pl.pallas_call(
        stats_kernel,
        out_shape=jax.ShapeDtypeStruct((16, rows), jnp.float32),
        in_specs=in_vmem(4),
        out_specs=pl.BlockSpec(memory_space=pltpu.VMEM),
        scratch_shapes=operand_scratch(rows, keys),
        compiler_params=pltpu.CompilerParams(vmem_limit_bytes=VMEM_LIMIT),
        cost_estimate=pl.CostEstimate(flops=2 * 10**9, bytes_accessed=4 * 10**6, transcendentals=10**6),
        name="stats",
    )(meta, qmeta, own, other, kv)


def grad_call(meta, qmeta, own, other, kv, stats, far):
    rows = own.shape[2] // HEAD * SPAN
    keys = kv.shape[0] * kv.shape[1]
    height, width = own.shape[1:]
    return pl.pallas_call(
        grad_kernel,
        out_shape=(
            jax.ShapeDtypeStruct((height, width), jnp.float32),
            jax.ShapeDtypeStruct((height, width), jnp.bfloat16),
            jax.ShapeDtypeStruct(kv.shape, jnp.bfloat16),
        ),
        in_specs=in_vmem(6),
        out_specs=[pl.BlockSpec(memory_space=pltpu.VMEM)] * 3,
        scratch_shapes=operand_scratch(rows, keys) + [
            pltpu.VMEM((keys // TILE, HEAD, TILE), jnp.bfloat16),
            pltpu.VMEM((keys, HEAD), jnp.float32),
            pltpu.VMEM((keys, HEAD), jnp.float32),
            pltpu.VMEM((HEAD, rows), jnp.float32),
            pltpu.VMEM((8, rows), jnp.float32),
        ],
        compiler_params=pltpu.CompilerParams(vmem_limit_bytes=VMEM_LIMIT),
        cost_estimate=pl.CostEstimate(flops=5 * 10**9, bytes_accessed=6 * 10**6, transcendentals=10**6),
        name="grads",
    )(meta, qmeta, own, other, kv, stats, far)


def reduce_copies_kernel(parts, copies, *halves):
    total = parts[0].astype(jnp.float32)
    for part in range(1, parts.shape[0]):
        total += parts[part].astype(jnp.float32)
    rounded = total.astype(copies.dtype)
    for copy in range(copies.shape[0]):
        copies[copy] = rounded
    for place, half in enumerate(halves):
        half[...] = rounded[:, place * HEAD:(place + 1) * HEAD]


def reduce_copies(parts, count, dtype, split, name):
    height, width = parts.shape[1:]
    halves = [jax.ShapeDtypeStruct((height, HEAD), dtype)] * (2 if split else 0)
    return pl.pallas_call(
        reduce_copies_kernel,
        out_shape=[jax.ShapeDtypeStruct((count, height, width), dtype)] + halves,
        in_specs=[pl.BlockSpec(memory_space=pltpu.VMEM)],
        out_specs=[pl.BlockSpec(memory_space=pltpu.VMEM)] * (1 + len(halves)),
        compiler_params=pltpu.CompilerParams(vmem_limit_bytes=VMEM_LIMIT),
        cost_estimate=pl.CostEstimate(flops=10**6, bytes_accessed=2 * 10**6, transcendentals=0),
        name=name,
    )(parts)


def weights_kernel(place, *refs):
    arrays, grads, out = refs[:-2], refs[-2], refs[-1]
    count = grads.shape[0] // 2
    rows = out.shape[1]
    slots = out.shape[0] // 2
    sources = [lax.rem(place[0] - back + count, count) * 2 for back in range(count)]
    here, there = place[2], 1 - place[2]
    right = jnp.concatenate([grads[s + here] for s in sources] + [grads[s + there] for s in sources], axis=0)
    each = len(arrays) // 2
    for high in range(2):
        blocks = [ref[i] for ref in arrays[high * each:(high + 1) * each] for i in range(ref.shape[0])]
        result = nn(jnp.concatenate(blocks, axis=1), right).astype(jnp.bfloat16)
        block = lax.bitwise_xor(place[1], high)
        for slot in range(slots):
            out[block * slots + slot] = result[slot * rows:(slot + 1) * rows]


def weights_call(place, arrays, grads, slots):
    rows = arrays[0].shape[1] // slots
    return pl.pallas_call(
        weights_kernel,
        out_shape=jax.ShapeDtypeStruct((2 * slots, rows, grads.shape[2]), jnp.bfloat16),
        in_specs=in_vmem(1 + len(arrays)),
        out_specs=pl.BlockSpec(memory_space=pltpu.VMEM),
        compiler_params=pltpu.CompilerParams(vmem_limit_bytes=VMEM_LIMIT),
        cost_estimate=pl.CostEstimate(flops=10**9, bytes_accessed=4 * 10**6, transcendentals=0),
        name="weights",
    )(place, *arrays, grads)


def around(array, axis, by):
    size = lax.axis_size(axis)
    return lax.ppermute(array, axis, [(i, (i + by) % size) for i in range(size)])


def swapped(array, axis):
    return lax.ppermute(array, axis, [(0, 1), (1, 0)])


def tables(doc_lengths, span_order):
    count = span_order.shape[0]
    outer, inner = lax.axis_size("ya"), lax.axis_size("z")
    side = lax.axis_index("yb")
    boundary = jnp.cumsum(doc_lengths[0])
    order = span_order.reshape(outer, 2, inner)
    mine = jnp.where(side == 0, order[:, 0], order[:, 1]).reshape(-1)
    spans = jnp.stack([mine, 2 * count - 1 - mine], axis=1).reshape(-1)
    rank = jnp.sum((spans[None, :] < spans[:, None]).astype(jnp.int32), axis=1)
    ctx = lax.axis_index(("ya", "yb", "z"))
    ids = jnp.arange(count, dtype=jnp.int32)
    first = jnp.sum(jnp.where(ids == ctx, span_order, 0))
    partner = ctx + (1 - 2 * side) * inner
    second = jnp.sum(jnp.where(ids == partner, span_order, 0))
    q_spans = jnp.stack([first, 2 * count - 1 - first, second, 2 * count - 1 - second])

    def doc_start(positions):
        reached = boundary <= positions[..., None]
        return jnp.max(jnp.where(reached, boundary, 0), axis=-1)

    low = doc_start(q_spans * SPAN) // SPAN
    lower = jnp.sum((spans[None, :] < low[:, None]).astype(jnp.int32), axis=1) // SPANS_PER_TILE
    upper = jnp.sum((spans[None, :] <= q_spans[:, None]).astype(jnp.int32), axis=1)
    upper = (upper + SPANS_PER_TILE - 1) // SPANS_PER_TILE
    bounds = jnp.concatenate([lower, upper, jnp.zeros((spans.shape[0] - 8,), jnp.int32)])
    meta = jnp.stack([rank, spans, bounds])
    return meta, q_spans, doc_start


def shards(queries, keys, values, out_grad, normed_input, doc_lengths, span_order):
    height = queries.shape[1]
    heads = queries.shape[2] // HEAD
    group = ("ya", "z")
    group_size = lax.axis_size("ya") * lax.axis_size("z")
    depth = lax.axis_size("z")

    own = jnp.concatenate([queries, out_grad], axis=0)
    other = swapped(own, "yb")
    pair = jnp.concatenate([keys[0], values[0]], axis=1)
    kv = lax.all_to_all(
        jnp.broadcast_to(pair[None], (group_size,) + pair.shape), group, 0, 0, tiled=True
    )

    meta, q_spans, doc_start = tables(doc_lengths, span_order)
    q_pos = q_spans[:, None] * SPAN + jnp.arange(SPAN, dtype=jnp.int32)[None, :]
    q_start = doc_start(q_pos)
    qmeta = jnp.tile(jnp.concatenate([q_pos, q_start], axis=0), (1, heads))

    other, features = lax.optimization_barrier((other, normed_input))
    copies_of = lax.axis_size("dp")
    replica = lax.axis_index("dp")
    rows = normed_input.shape[2] // (depth * copies_of)
    slabs = features[0].reshape(height, depth, copies_of, rows).transpose(2, 1, 3, 0)
    slabs = slabs.reshape(copies_of, depth * rows, height)
    columns = []
    for by in range(copies_of):
        place = lax.rem(replica + by, copies_of)
        slab = lax.dynamic_index_in_dim(slabs, place, 0, keepdims=False)
        columns.append(
            lax.ppermute(
                slab,
                ("dp", "yb", "core"),
                [
                    (d * 4 + b * 2 + c, (d + by) % copies_of * 4 + c * 2 + b)
                    for d in range(copies_of) for b in range(2) for c in range(2)
                ],
            )
        )
    half = copies_of // 2
    near = jnp.stack(columns[:half]), jnp.stack(columns[half:])

    beside_a = swapped(near[0], "yh")
    stats = stats_call(meta, qmeta, own, other, kv)
    stats, near_b = lax.optimization_barrier((stats, near[1]))
    beside_b = swapped(near_b, "yh")
    far = swapped(stats, "yb")
    far, beside_a = lax.optimization_barrier((far, beside_a))
    dq_own, dq_other, dkv = grad_call(meta, qmeta, own, other, kv, stats, far)
    dkv, beside_b = lax.optimization_barrier((dkv, beside_b))
    near, beside = [near[0], near_b], [beside_a, beside_b]
    dq_far = swapped(dq_other, "yb")
    across = [swapped(part, "core") for part in (*near, *beside)]
    parts = lax.all_to_all(dkv, group, 0, 0, tiled=True)
    parts, across, dq_far = lax.optimization_barrier((parts, across, dq_far))
    copies, key_grad, value_grad = reduce_copies(parts, 2 * copies_of, jnp.bfloat16, True, "sum_grads")
    query_grad = (dq_own + dq_far.astype(jnp.float32)).astype(jnp.bfloat16)[None]

    all_grads = lax.all_to_all(copies, ("dp", "yb"), 0, 0, tiled=True)
    place = jnp.stack([replica, lax.axis_index("yh"), lax.axis_index("core")]).astype(jnp.int32)
    blocks = weights_call(place, (*near, *across[:2], *beside, *across[2:]), all_grads, depth)
    pieces = lax.all_to_all(blocks, group, 0, 0, tiled=True)
    (spread,) = reduce_copies(pieces, copies_of, jnp.float32, False, "sum_rows")
    weight = lax.all_to_all(spread, "dp", 0, 0, tiled=True).reshape(copies_of * rows, 2 * HEAD)
    return (query_grad, key_grad[None], value_grad[None], weight[:, :HEAD], weight[:, HEAD:])


def solution(mesh):
    sizes = dict(mesh.shape)
    deep = sizes["ctx"] // 4
    fine = Mesh(
        mesh.devices.reshape(sizes["dp"], 2, 2, deep, 2, sizes["tp"] // 2),
        ("dp", "ya", "yb", "z", "yh", "core"),
    )
    context, model = ("ya", "yb", "z"), ("yh", "core")
    in_specs = (
        P("dp", context, model),
        P("dp", context, model),
        P("dp", context, model),
        P("dp", context, model),
        P("dp", context, model),
        P("dp", None),
        P(),
    )
    out_specs = (
        P("dp", context, model),
        P("dp", context, model),
        P("dp", context, model),
        P(context, model),
        P(context, model),
    )
    return jax.shard_map(shards, mesh=fine, in_specs=in_specs, out_specs=out_specs, check_vma=False)
```

```python
import jax
import jax.numpy as jnp
from jax import lax
from jax.experimental import pallas as pl
from jax.experimental.pallas import tpu as pltpu
from jax.sharding import Mesh, PartitionSpec as P

HEAD = 128
SPAN = 64
TILE = 256
SPANS_PER_TILE = TILE // SPAN
NEG = -1e30
SCALE = HEAD ** (-0.5)
LOG2E = 1.4426950408889634
VMEM_LIMIT = 24 * 1024 * 1024
SMALL_LIMIT = 12 * 1024 * 1024


def nt(left, right):
    return lax.dot_general(left, right, (((1,), (1,)), ((), ())), preferred_element_type=jnp.float32)


def nn(left, right):
    return lax.dot_general(left, right, (((1,), (0,)), ((), ())), preferred_element_type=jnp.float32)


def queries_kernel(own, other, q_s, g_s, qt_s, gt_s):
    heads = own.shape[2] // HEAD
    rows = heads * SPAN
    for source, block in enumerate((own, other)):
        for half in range(2):
            u = source * 2 + half
            for which, plain, turned in ((0, q_s, qt_s), (1, g_s, gt_s)):
                pieces = [
                    block[which, half * SPAN:(half + 1) * SPAN, head * HEAD:(head + 1) * HEAD] for head in range(heads)
                ]
                laid = jnp.concatenate(pieces, axis=0)
                plain[u * rows:(u + 1) * rows, :] = laid
                turned[u] = laid.T


def queries_call(own, other):
    rows = own.shape[2] // HEAD * SPAN
    plain = jax.ShapeDtypeStruct((4 * rows, HEAD), jnp.bfloat16)
    turned = jax.ShapeDtypeStruct((4, HEAD, rows), jnp.bfloat16)
    return pl.pallas_call(
        queries_kernel,
        out_shape=[plain, plain, turned, turned],
        in_specs=[pl.BlockSpec(memory_space=pltpu.VMEM)] * 2,
        out_specs=[pl.BlockSpec(memory_space=pltpu.VMEM)] * 4,
        compiler_params=pltpu.CompilerParams(vmem_limit_bytes=SMALL_LIMIT),
        cost_estimate=pl.CostEstimate(flops=10**6, bytes_accessed=3 * 10**6, transcendentals=0),
        name="queries",
    )(own, other)


def place_keys(meta, kv, k_s, v_s, pos_s):
    lane_rows = lax.broadcasted_iota(jnp.int32, (SPAN, 128), 0)

    def place(block, carry):
        for half in range(2):
            span = 2 * block + half
            start = pl.multiple_of(meta[0, span] * SPAN, SPAN)
            piece = kv[block, half * SPAN:(half + 1) * SPAN, :]
            k_s[pl.ds(start, SPAN), :] = piece[:, :HEAD]
            v_s[pl.ds(start, SPAN), :] = piece[:, HEAD:]
            pos_s[pl.ds(start, SPAN), :] = lane_rows + meta[1, span] * SPAN
        return carry

    lax.fori_loop(0, kv.shape[0], place, 0)


def masked_scores(k_tile, q_cols, pos_tile, q_pos, q_start):
    copies = q_cols.shape[1] // 128
    key_pos = jnp.concatenate([pos_tile] * copies, axis=1)
    mask = (key_pos <= q_pos) & (key_pos >= q_start)
    return jnp.where(mask, nn(k_tile, q_cols) * (SCALE * LOG2E), NEG)


def list_tiles(meta, items, together):
    def add(t, n, u):
        items[n] = u * 32 + t
        return n + 1

    count = jnp.int32(0)
    for u in range(4):
        count = lax.fori_loop(meta[2, u], meta[2, 4 + u], lambda t, n, u=u: add(t, n, u), count)
    for spare in range(together - 1):
        items[count + spare] = 4 * 32
    return lax.div(count + together - 1, together)


def tile_scores(item, qmeta, qt_s, k_s, pos_s):
    u, t = lax.shift_right_logical(item, 5), item & 31
    here = pl.ds(pl.multiple_of(t * TILE, TILE), TILE)
    span = lax.rem(u, 4)
    scores = masked_scores(
        k_s[here, :], qt_s[span], pos_s[here, :], qmeta[pl.ds(2 * u, 1), :], qmeta[pl.ds(2 * u + 1, 1), :]
    )
    return span, here, t, scores


def stats_kernel(meta, qmeta, qt_s, gt_s, kv, out, k_s, v_s, pos_s, items):
    place_keys(meta, kv, k_s, v_s, pos_s)
    rows = qt_s.shape[2]
    out[0:4, :] = jnp.full((4, rows), NEG, jnp.float32)
    out[4:16, :] = jnp.zeros((12, rows), jnp.float32)
    groups = list_tiles(meta, items, 2)

    def group_step(group, carry):
        found = []
        for slot in range(2):
            span, here, t, scores = tile_scores(items[group * 2 + slot], qmeta, qt_s, k_s, pos_s)
            top = jnp.max(scores, axis=0, keepdims=True)
            probs = jnp.exp2(scores - top)
            grad = nn(v_s[here, :], gt_s[span])
            total = jnp.sum(probs, axis=0, keepdims=True)
            found.append((span, top, total, jnp.sum(probs * grad, axis=0, keepdims=True)))
        for span, top, total, weighted in found:
            before = out[pl.ds(span, 1), :]
            new_top = jnp.maximum(before, top)
            keep, scale = jnp.exp2(before - new_top), jnp.exp2(top - new_top)
            out[pl.ds(span, 1), :] = new_top
            out[pl.ds(4 + span, 1), :] = keep * out[pl.ds(4 + span, 1), :] + scale * total
            out[pl.ds(8 + span, 1), :] = keep * out[pl.ds(8 + span, 1), :] + scale * weighted
        return carry

    lax.fori_loop(0, groups, group_step, 0)


def grad_kernel(
    meta, qmeta, q_s, g_s, qt_s, gt_s, k_s, v_s, pos_s, stats, far, dq_own, dq_other, dkv,
    items, kt_s, dk_s, dv_s, dq_s, fin_s,
):
    rows = q_s.shape[0] // 4
    heads = rows // SPAN
    tiles = k_s.shape[0] // TILE
    for t in range(tiles):
        kt_s[t] = k_s[t * TILE:(t + 1) * TILE, :].T
    dk_s[...] = jnp.zeros_like(dk_s)
    dv_s[...] = jnp.zeros_like(dv_s)
    dq_s[...] = jnp.zeros_like(dq_s)
    for u in range(4):
        v = (u + 2) % 4
        top_a, top_b = stats[u:u + 1, :], far[v:v + 1, :]
        top = jnp.maximum(top_a, top_b)
        scale_a, scale_b = jnp.exp2(top_a - top), jnp.exp2(top_b - top)
        total = scale_a * stats[4 + u:5 + u, :] + scale_b * far[4 + v:5 + v, :]
        weighted = scale_a * stats[8 + u:9 + u, :] + scale_b * far[8 + v:9 + v, :]
        fin_s[u:u + 1, :] = top + jnp.log(total) * LOG2E
        fin_s[4 + u:5 + u, :] = weighted / total
    groups = list_tiles(meta, items, 2)

    def group_step(group, carry):
        found = []
        for slot in range(2):
            span, here, t, scores = tile_scores(items[group * 2 + slot], qmeta, qt_s, k_s, pos_s)
            probs = jnp.exp2(scores - fin_s[pl.ds(span, 1), :])
            grad = nn(v_s[here, :], gt_s[span])
            score_grad = (probs * (grad - fin_s[pl.ds(4 + span, 1), :])).astype(jnp.bfloat16)
            base = pl.ds(pl.multiple_of(span * rows, rows), rows)
            found.append((
                span, here, nn(probs.astype(jnp.bfloat16), g_s[base, :]), nn(score_grad, q_s[base, :]),
                nn(kt_s[t], score_grad),
            ))
        for span, here, value_part, key_part, query_part in found:
            dv_s[here, :] += value_part
            dk_s[here, :] += key_part
            dq_s[span] += query_part
        return carry

    lax.fori_loop(0, groups, group_step, 0)
    for u in range(4):
        flat = (dq_s[u] * SCALE).T
        half = (u % 2) * SPAN
        for head in range(heads):
            piece = flat[head * SPAN:(head + 1) * SPAN, :]
            if u < 2:
                dq_own[half:half + SPAN, head * HEAD:(head + 1) * HEAD] = piece
            else:
                dq_other[half:half + SPAN, head * HEAD:(head + 1) * HEAD] = piece.astype(jnp.bfloat16)

    def unplace(block, carry):
        for half in range(2):
            start = pl.multiple_of(meta[0, 2 * block + half] * SPAN, SPAN)
            here = pl.ds(start, SPAN)
            dkv[block, half * SPAN:(half + 1) * SPAN, :HEAD] = (dk_s[here, :] * SCALE).astype(jnp.bfloat16)
            dkv[block, half * SPAN:(half + 1) * SPAN, HEAD:] = dv_s[here, :].astype(jnp.bfloat16)
        return carry

    lax.fori_loop(0, dkv.shape[0], unplace, 0)


def item_scratch(keys):
    return pltpu.SMEM((4 * (keys // TILE) + 8,), jnp.int32)


def in_vmem(count):
    return [pl.BlockSpec(memory_space=pltpu.SMEM)] + [pl.BlockSpec(memory_space=pltpu.VMEM)] * count


def stats_call(meta, qmeta, turned, kv):
    rows = turned[0].shape[2]
    keys = kv.shape[0] * kv.shape[1]
    sorted_keys = jax.ShapeDtypeStruct((keys, HEAD), jnp.bfloat16)
    return pl.pallas_call(
        stats_kernel,
        out_shape=[
            jax.ShapeDtypeStruct((16, rows), jnp.float32),
            sorted_keys,
            sorted_keys,
            jax.ShapeDtypeStruct((keys, 128), jnp.int32),
        ],
        in_specs=in_vmem(4),
        out_specs=[pl.BlockSpec(memory_space=pltpu.VMEM)] * 4,
        scratch_shapes=[item_scratch(keys)],
        compiler_params=pltpu.CompilerParams(vmem_limit_bytes=VMEM_LIMIT),
        cost_estimate=pl.CostEstimate(flops=2 * 10**9, bytes_accessed=4 * 10**6, transcendentals=10**6),
        name="stats",
    )(meta, qmeta, *turned, kv)


def grad_call(meta, qmeta, laid, turned, placed, stats, far, shape, heads):
    rows = turned[0].shape[2]
    keys = shape[0] * shape[1]
    height, width = 2 * SPAN, heads * HEAD
    return pl.pallas_call(
        grad_kernel,
        out_shape=(
            jax.ShapeDtypeStruct((height, width), jnp.float32),
            jax.ShapeDtypeStruct((height, width), jnp.bfloat16),
            jax.ShapeDtypeStruct(shape, jnp.bfloat16),
        ),
        in_specs=in_vmem(10),
        out_specs=[pl.BlockSpec(memory_space=pltpu.VMEM)] * 3,
        scratch_shapes=[
            item_scratch(keys),
            pltpu.VMEM((keys // TILE, HEAD, TILE), jnp.bfloat16),
            pltpu.VMEM((keys, HEAD), jnp.float32),
            pltpu.VMEM((keys, HEAD), jnp.float32),
            pltpu.VMEM((4, HEAD, rows), jnp.float32),
            pltpu.VMEM((8, rows), jnp.float32),
        ],
        compiler_params=pltpu.CompilerParams(vmem_limit_bytes=VMEM_LIMIT),
        cost_estimate=pl.CostEstimate(flops=5 * 10**9, bytes_accessed=6 * 10**6, transcendentals=10**6),
        name="grads",
    )(meta, qmeta, *laid, *turned, *placed, stats, far)


def reduce_copies_kernel(parts, copies, *halves):
    total = parts[0].astype(jnp.float32)
    for part in range(1, parts.shape[0]):
        total += parts[part].astype(jnp.float32)
    rounded = total.astype(copies.dtype)
    for copy in range(copies.shape[0]):
        copies[copy] = rounded
    for place, half in enumerate(halves):
        half[...] = rounded[:, place * HEAD:(place + 1) * HEAD]


def reduce_copies(parts, count, dtype, split, name):
    height, width = parts.shape[1:]
    halves = [jax.ShapeDtypeStruct((height, HEAD), dtype)] * (2 if split else 0)
    return pl.pallas_call(
        reduce_copies_kernel,
        out_shape=[jax.ShapeDtypeStruct((count, height, width), dtype)] + halves,
        in_specs=[pl.BlockSpec(memory_space=pltpu.VMEM)],
        out_specs=[pl.BlockSpec(memory_space=pltpu.VMEM)] * (1 + len(halves)),
        compiler_params=pltpu.CompilerParams(vmem_limit_bytes=SMALL_LIMIT),
        cost_estimate=pl.CostEstimate(flops=10**6, bytes_accessed=2 * 10**6, transcendentals=0),
        name=name,
    )(parts)


def weights_kernel(place, *refs):
    arrays, grads, out = refs[:-2], refs[-2], refs[-1]
    count = grads.shape[0] // 2
    rows = out.shape[1]
    slots = out.shape[0] // 2
    sources = [lax.rem(place[0] - back + count, count) * 2 for back in range(count)]
    here, there = place[2], 1 - place[2]
    right = jnp.concatenate([grads[s + here] for s in sources] + [grads[s + there] for s in sources], axis=0)
    each = len(arrays) // 2
    for high in range(2):
        blocks = [ref[i] for ref in arrays[high * each:(high + 1) * each] for i in range(ref.shape[0])]
        result = nn(jnp.concatenate(blocks, axis=1), right).astype(jnp.bfloat16)
        block = lax.bitwise_xor(place[1], high)
        for slot in range(slots):
            out[block * slots + slot] = result[slot * rows:(slot + 1) * rows]


def weights_call(place, arrays, grads, slots):
    rows = arrays[0].shape[1] // slots
    return pl.pallas_call(
        weights_kernel,
        out_shape=jax.ShapeDtypeStruct((2 * slots, rows, grads.shape[2]), jnp.bfloat16),
        in_specs=in_vmem(1 + len(arrays)),
        out_specs=pl.BlockSpec(memory_space=pltpu.VMEM),
        compiler_params=pltpu.CompilerParams(vmem_limit_bytes=SMALL_LIMIT),
        cost_estimate=pl.CostEstimate(flops=10**9, bytes_accessed=4 * 10**6, transcendentals=0),
        name="weights",
    )(place, *arrays, grads)


def around(array, axis, by):
    size = lax.axis_size(axis)
    return lax.ppermute(array, axis, [(i, (i + by) % size) for i in range(size)])


def swapped(array, axis):
    return lax.ppermute(array, axis, [(0, 1), (1, 0)])


def tables(doc_lengths, span_order):
    count = span_order.shape[0]
    outer, inner = lax.axis_size("ya"), lax.axis_size("z")
    side = lax.axis_index("yb")
    boundary = jnp.cumsum(doc_lengths[0])
    order = span_order.reshape(outer, 2, inner)
    mine = jnp.where(side == 0, order[:, 0], order[:, 1]).reshape(-1)
    spans = jnp.stack([mine, 2 * count - 1 - mine], axis=1).reshape(-1)
    rank = jnp.sum((spans[None, :] < spans[:, None]).astype(jnp.int32), axis=1)
    ctx = lax.axis_index(("ya", "yb", "z"))
    ids = jnp.arange(count, dtype=jnp.int32)
    first = jnp.sum(jnp.where(ids == ctx, span_order, 0))
    partner = ctx + (1 - 2 * side) * inner
    second = jnp.sum(jnp.where(ids == partner, span_order, 0))
    q_spans = jnp.stack([first, 2 * count - 1 - first, second, 2 * count - 1 - second])

    def doc_start(positions):
        reached = boundary <= positions[..., None]
        return jnp.max(jnp.where(reached, boundary, 0), axis=-1)

    low = doc_start(q_spans * SPAN) // SPAN
    lower = jnp.sum((spans[None, :] < low[:, None]).astype(jnp.int32), axis=1) // SPANS_PER_TILE
    upper = jnp.sum((spans[None, :] <= q_spans[:, None]).astype(jnp.int32), axis=1)
    upper = (upper + SPANS_PER_TILE - 1) // SPANS_PER_TILE
    bounds = jnp.concatenate([lower, upper, jnp.zeros((spans.shape[0] - 8,), jnp.int32)])
    meta = jnp.stack([rank, spans, bounds])
    return meta, q_spans, doc_start


def shards(queries, keys, values, out_grad, normed_input, doc_lengths, span_order):
    height = queries.shape[1]
    heads = queries.shape[2] // HEAD
    group = ("ya", "z")
    group_size = lax.axis_size("ya") * lax.axis_size("z")
    depth = lax.axis_size("z")

    own = jnp.concatenate([queries, out_grad], axis=0)
    other = swapped(own, "yb")
    pair = jnp.concatenate([keys[0], values[0]], axis=1)
    kv = lax.all_to_all(
        jnp.broadcast_to(pair[None], (group_size,) + pair.shape), group, 0, 0, tiled=True
    )

    meta, q_spans, doc_start = tables(doc_lengths, span_order)
    q_pos = q_spans[:, None] * SPAN + jnp.arange(SPAN, dtype=jnp.int32)[None, :]
    q_start = doc_start(q_pos)
    qmeta = jnp.pad(jnp.stack([q_pos, q_start], axis=1).reshape(8, SPAN), ((0, 8), (0, 0)), constant_values=-1)
    qmeta = jnp.tile(qmeta, (1, heads))

    other, features = lax.optimization_barrier((other, normed_input))
    copies_of = lax.axis_size("dp")
    replica = lax.axis_index("dp")
    rows = normed_input.shape[2] // (depth * copies_of)
    slabs = features[0].reshape(height, depth, copies_of, rows).transpose(2, 1, 3, 0)
    slabs = slabs.reshape(copies_of, depth * rows, height)
    columns = []
    for by in range(copies_of):
        place = lax.rem(replica + by, copies_of)
        slab = lax.dynamic_index_in_dim(slabs, place, 0, keepdims=False)
        columns.append(
            lax.ppermute(
                slab,
                ("dp", "yb", "core"),
                [
                    (d * 4 + b * 2 + c, (d + by) % copies_of * 4 + c * 2 + b)
                    for d in range(copies_of) for b in range(2) for c in range(2)
                ],
            )
        )
    half = copies_of // 2
    near_a = jnp.stack(columns[:half])

    beside_a = swapped(near_a, "yh")
    *laid, qt, gt = queries_call(own, other)
    stats, *placed = stats_call(meta, qmeta, (qt, gt), kv)
    stats, columns = lax.optimization_barrier((stats, columns[half:]))
    near_b = jnp.stack(columns)
    beside_b = swapped(near_b, "yh")
    far = swapped(stats, "yb")
    far, beside_a = lax.optimization_barrier((far, beside_a))
    dq_own, dq_other, dkv = grad_call(meta, qmeta, laid, (qt, gt), placed, stats, far, kv.shape, heads)
    dkv, beside_b = lax.optimization_barrier((dkv, beside_b))
    near, beside = [near_a, near_b], [beside_a, beside_b]
    dq_far = swapped(dq_other, "yb")
    across = [swapped(part, "core") for part in (*near, *beside)]
    parts = lax.all_to_all(dkv, group, 0, 0, tiled=True)
    parts, across, dq_far = lax.optimization_barrier((parts, across, dq_far))
    copies, key_grad, value_grad = reduce_copies(parts, 2 * copies_of, jnp.bfloat16, True, "sum_grads")
    query_grad = (dq_own + dq_far.astype(jnp.float32)).astype(jnp.bfloat16)[None]

    all_grads = lax.all_to_all(copies, ("dp", "yb"), 0, 0, tiled=True)
    place = jnp.stack([replica, lax.axis_index("yh"), lax.axis_index("core")]).astype(jnp.int32)
    blocks = weights_call(place, (*near, *across[:2], *beside, *across[2:]), all_grads, depth)
    pieces = lax.all_to_all(blocks, group, 0, 0, tiled=True)
    (spread,) = reduce_copies(pieces, copies_of, jnp.float32, False, "sum_rows")
    weight = lax.all_to_all(spread, "dp", 0, 0, tiled=True).reshape(copies_of * rows, 2 * HEAD)
    return (query_grad, key_grad[None], value_grad[None], weight[:, :HEAD], weight[:, HEAD:])


def solution(mesh):
    sizes = dict(mesh.shape)
    deep = sizes["ctx"] // 4
    fine = Mesh(
        mesh.devices.reshape(sizes["dp"], 2, 2, deep, 2, sizes["tp"] // 2),
        ("dp", "ya", "yb", "z", "yh", "core"),
    )
    context, model = ("ya", "yb", "z"), ("yh", "core")
    in_specs = (
        P("dp", context, model),
        P("dp", context, model),
        P("dp", context, model),
        P("dp", context, model),
        P("dp", context, model),
        P("dp", None),
        P(),
    )
    out_specs = (
        P("dp", context, model),
        P("dp", context, model),
        P("dp", context, model),
        P(context, model),
        P(context, model),
    )
    return jax.shard_map(shards, mesh=fine, in_specs=in_specs, out_specs=out_specs, check_vma=False)
```

```python
import jax
import jax.numpy as jnp
from jax import lax
from jax.experimental import pallas as pl
from jax.experimental.pallas import tpu as pltpu
from jax.sharding import Mesh, PartitionSpec as P

HEAD = 128
SPAN = 64
TILE = 256
SPANS_PER_TILE = TILE // SPAN
NEG = -1e30
SCALE = HEAD ** (-0.5)
LOG2E = 1.4426950408889634
VMEM_LIMIT = 24 * 1024 * 1024
SMALL_LIMIT = 12 * 1024 * 1024


def nt(left, right):
    return lax.dot_general(left, right, (((1,), (1,)), ((), ())), preferred_element_type=jnp.float32)


def nn(left, right):
    return lax.dot_general(left, right, (((1,), (0,)), ((), ())), preferred_element_type=jnp.float32)


def load_operands(meta, own, other, kv, q_s, g_s, k_s, v_s, pos_s):
    rows = own.shape[1]
    for source, block in enumerate((own, other)):
        q_s[source * rows:(source + 1) * rows, :] = block[0]
        g_s[source * rows:(source + 1) * rows, :] = block[1]
    lane_rows = lax.broadcasted_iota(jnp.int32, (SPAN, 128), 0)

    def place(block, carry):
        for half in range(2):
            span = 2 * block + half
            start = pl.multiple_of(meta[0, span] * SPAN, SPAN)
            piece = kv[block, half * SPAN:(half + 1) * SPAN, :]
            k_s[pl.ds(start, SPAN), :] = piece[:, :HEAD]
            v_s[pl.ds(start, SPAN), :] = piece[:, HEAD:]
            pos_s[pl.ds(start, SPAN), :] = lane_rows + meta[1, span] * SPAN
        return carry

    lax.fori_loop(0, kv.shape[0], place, 0)


def masked_scores(k_tile, q_rows, pos_tile, q_pos, q_start):
    copies = q_rows.shape[0] // 128
    key_pos = jnp.concatenate([pos_tile] * copies, axis=1)
    mask = (key_pos <= q_pos) & (key_pos >= q_start)
    return jnp.where(mask, nt(k_tile, q_rows) * (SCALE * LOG2E), NEG)


def list_tiles(meta, items, together):
    def add(t, n, u):
        items[n] = u * 32 + t
        return n + 1

    count = jnp.int32(0)
    for u in range(4):
        count = lax.fori_loop(meta[2, u], meta[2, 4 + u], lambda t, n, u=u: add(t, n, u), count)
    for spare in range(together - 1):
        items[count + spare] = 4 * 32
    return lax.div(count + together - 1, together)


def tile_scores(item, qmeta, q_s, k_s, pos_s):
    u, t = lax.shift_right_logical(item, 5), item & 31
    here = pl.ds(pl.multiple_of(t * TILE, TILE), TILE)
    span = lax.rem(u, 4)
    rows = qmeta.shape[1]
    base = pl.ds(pl.multiple_of(span * rows, rows), rows)
    scores = masked_scores(
        k_s[here, :], q_s[base, :], pos_s[here, :], qmeta[pl.ds(2 * u, 1), :], qmeta[pl.ds(2 * u + 1, 1), :]
    )
    return span, base, here, t, scores


def stats_kernel(meta, qmeta, own, other, kv, out, q_s, g_s, k_s, v_s, pos_s, items):
    load_operands(meta, own, other, kv, q_s, g_s, k_s, v_s, pos_s)
    rows = qmeta.shape[1]
    out[0:4, :] = jnp.full((4, rows), NEG, jnp.float32)
    out[4:16, :] = jnp.zeros((12, rows), jnp.float32)
    groups = list_tiles(meta, items, 2)

    def group_step(group, carry):
        found = []
        for slot in range(2):
            span, base, here, t, scores = tile_scores(items[group * 2 + slot], qmeta, q_s, k_s, pos_s)
            top = jnp.max(scores, axis=0, keepdims=True)
            probs = jnp.exp2(scores - top)
            grad = nt(v_s[here, :], g_s[base, :])
            total = jnp.sum(probs, axis=0, keepdims=True)
            found.append((span, top, total, jnp.sum(probs * grad, axis=0, keepdims=True)))
        for span, top, total, weighted in found:
            before = out[pl.ds(span, 1), :]
            new_top = jnp.maximum(before, top)
            keep, scale = jnp.exp2(before - new_top), jnp.exp2(top - new_top)
            out[pl.ds(span, 1), :] = new_top
            out[pl.ds(4 + span, 1), :] = keep * out[pl.ds(4 + span, 1), :] + scale * total
            out[pl.ds(8 + span, 1), :] = keep * out[pl.ds(8 + span, 1), :] + scale * weighted
        return carry

    lax.fori_loop(0, groups, group_step, 0)


def grad_kernel(
    meta, qmeta, own, other, kv, stats, far, dq_own, dq_other, dkv,
    q_s, g_s, k_s, v_s, pos_s, items, kt_s, dk_s, dv_s, dq_s, fin_s,
):
    load_operands(meta, own, other, kv, q_s, g_s, k_s, v_s, pos_s)
    rows = qmeta.shape[1]
    heads = rows // SPAN
    tiles = k_s.shape[0] // TILE
    for t in range(tiles):
        kt_s[t] = k_s[t * TILE:(t + 1) * TILE, :].T
    dk_s[...] = jnp.zeros_like(dk_s)
    dv_s[...] = jnp.zeros_like(dv_s)
    dq_s[...] = jnp.zeros_like(dq_s)
    for u in range(4):
        v = (u + 2) % 4
        top_a, top_b = stats[u:u + 1, :], far[v:v + 1, :]
        top = jnp.maximum(top_a, top_b)
        scale_a, scale_b = jnp.exp2(top_a - top), jnp.exp2(top_b - top)
        total = scale_a * stats[4 + u:5 + u, :] + scale_b * far[4 + v:5 + v, :]
        weighted = scale_a * stats[8 + u:9 + u, :] + scale_b * far[8 + v:9 + v, :]
        fin_s[u:u + 1, :] = top + jnp.log(total) * LOG2E
        fin_s[4 + u:5 + u, :] = weighted / total
    groups = list_tiles(meta, items, 2)

    def group_step(group, carry):
        found = []
        for slot in range(2):
            span, base, here, t, scores = tile_scores(items[group * 2 + slot], qmeta, q_s, k_s, pos_s)
            probs = jnp.exp2(scores - fin_s[pl.ds(span, 1), :])
            grad = nt(v_s[here, :], g_s[base, :])
            score_grad = (probs * (grad - fin_s[pl.ds(4 + span, 1), :])).astype(jnp.bfloat16)
            found.append((
                span, here, nn(probs.astype(jnp.bfloat16), g_s[base, :]), nn(score_grad, q_s[base, :]),
                nn(kt_s[t], score_grad),
            ))
        for span, here, value_part, key_part, query_part in found:
            dv_s[here, :] += value_part
            dk_s[here, :] += key_part
            dq_s[span] += query_part
        return carry

    lax.fori_loop(0, groups, group_step, 0)
    for u in range(4):
        flat = (dq_s[u] * SCALE).T
        half = (u % 2) * SPAN
        for head in range(heads):
            piece = flat[head * SPAN:(head + 1) * SPAN, :]
            if u < 2:
                dq_own[half:half + SPAN, head * HEAD:(head + 1) * HEAD] = piece
            else:
                dq_other[half:half + SPAN, head * HEAD:(head + 1) * HEAD] = piece.astype(jnp.bfloat16)

    depth = dkv.shape[0] // 2

    def unplace(block, carry):
        for half in range(2):
            start = pl.multiple_of(meta[0, 2 * block + half] * SPAN, SPAN)
            here = pl.ds(start, SPAN)
            there = lax.rem(block, depth) * 2 + lax.div(block, depth)
            dkv[there, half * SPAN:(half + 1) * SPAN, :HEAD] = (dk_s[here, :] * SCALE).astype(jnp.bfloat16)
            dkv[there, half * SPAN:(half + 1) * SPAN, HEAD:] = dv_s[here, :].astype(jnp.bfloat16)
        return carry

    lax.fori_loop(0, dkv.shape[0], unplace, 0)


def operand_scratch(rows, keys):
    return [
        pltpu.VMEM((4 * rows, HEAD), jnp.bfloat16),
        pltpu.VMEM((4 * rows, HEAD), jnp.bfloat16),
        pltpu.VMEM((keys, HEAD), jnp.bfloat16),
        pltpu.VMEM((keys, HEAD), jnp.bfloat16),
        pltpu.VMEM((keys, 128), jnp.int32),
        pltpu.SMEM((4 * (keys // TILE) + 8,), jnp.int32),
    ]


def in_vmem(count):
    return [pl.BlockSpec(memory_space=pltpu.SMEM)] + [pl.BlockSpec(memory_space=pltpu.VMEM)] * count


def stats_call(meta, qmeta, own, other, kv):
    rows = qmeta.shape[1]
    keys = kv.shape[0] * kv.shape[1]
    return pl.pallas_call(
        stats_kernel,
        out_shape=jax.ShapeDtypeStruct((16, rows), jnp.float32),
        in_specs=in_vmem(4),
        out_specs=pl.BlockSpec(memory_space=pltpu.VMEM),
        scratch_shapes=operand_scratch(rows, keys),
        compiler_params=pltpu.CompilerParams(vmem_limit_bytes=VMEM_LIMIT),
        cost_estimate=pl.CostEstimate(flops=2 * 10**9, bytes_accessed=4 * 10**6, transcendentals=10**6),
        name="stats",
    )(meta, qmeta, own, other, kv)


def grad_call(meta, qmeta, own, other, kv, stats, far):
    rows = qmeta.shape[1]
    keys = kv.shape[0] * kv.shape[1]
    height, width = 2 * SPAN, rows // SPAN * HEAD
    return pl.pallas_call(
        grad_kernel,
        out_shape=(
            jax.ShapeDtypeStruct((height, width), jnp.float32),
            jax.ShapeDtypeStruct((height, width), jnp.bfloat16),
            jax.ShapeDtypeStruct(kv.shape, jnp.bfloat16),
        ),
        in_specs=in_vmem(6),
        out_specs=[pl.BlockSpec(memory_space=pltpu.VMEM)] * 3,
        scratch_shapes=operand_scratch(rows, keys) + [
            pltpu.VMEM((keys // TILE, HEAD, TILE), jnp.bfloat16),
            pltpu.VMEM((keys, HEAD), jnp.float32),
            pltpu.VMEM((keys, HEAD), jnp.float32),
            pltpu.VMEM((4, HEAD, rows), jnp.float32),
            pltpu.VMEM((8, rows), jnp.float32),
        ],
        compiler_params=pltpu.CompilerParams(vmem_limit_bytes=VMEM_LIMIT),
        cost_estimate=pl.CostEstimate(flops=5 * 10**9, bytes_accessed=6 * 10**6, transcendentals=10**6),
        name="grads",
    )(meta, qmeta, own, other, kv, stats, far)


def first_sum_kernel(place, parts, kept, sent):
    for where, out in ((place[3], kept), (1 - place[3], sent)):
        total = parts[where].astype(jnp.float32)
        for level in range(1, parts.shape[0] // 2):
            total += parts[2 * level + where].astype(jnp.float32)
        out[...] = total.astype(out.dtype)


def first_sum(place, parts):
    shape = parts.shape[1:]
    return pl.pallas_call(
        first_sum_kernel,
        out_shape=[jax.ShapeDtypeStruct(shape, jnp.float32), jax.ShapeDtypeStruct(shape, jnp.bfloat16)],
        in_specs=in_vmem(1),
        out_specs=[pl.BlockSpec(memory_space=pltpu.VMEM)] * 2,
        compiler_params=pltpu.CompilerParams(vmem_limit_bytes=SMALL_LIMIT),
        cost_estimate=pl.CostEstimate(flops=10**6, bytes_accessed=2 * 10**6, transcendentals=0),
        name="first_sum",
    )(place, parts)


def second_sum_kernel(kept, got, copies, key_out, value_out):
    rounded = (kept[...] + got[...].astype(jnp.float32)).astype(jnp.bfloat16)
    for copy in range(copies.shape[0]):
        copies[copy] = rounded
    key_out[...] = rounded[:, :HEAD]
    value_out[...] = rounded[:, HEAD:]


def second_sum(kept, got, count):
    height, width = kept.shape
    half = jax.ShapeDtypeStruct((height, HEAD), jnp.bfloat16)
    return pl.pallas_call(
        second_sum_kernel,
        out_shape=[jax.ShapeDtypeStruct((count, height, width), jnp.bfloat16), half, half],
        in_specs=[pl.BlockSpec(memory_space=pltpu.VMEM)] * 2,
        out_specs=[pl.BlockSpec(memory_space=pltpu.VMEM)] * 3,
        compiler_params=pltpu.CompilerParams(vmem_limit_bytes=SMALL_LIMIT),
        cost_estimate=pl.CostEstimate(flops=10**6, bytes_accessed=10**6, transcendentals=0),
        name="second_sum",
    )(kept, got)


def sum_rows_kernel(parts, copies):
    total = parts[0].astype(jnp.float32)
    for part in range(1, parts.shape[0]):
        total += parts[part].astype(jnp.float32)
    for copy in range(copies.shape[0]):
        copies[copy] = total


def sum_rows(parts, count):
    return pl.pallas_call(
        sum_rows_kernel,
        out_shape=jax.ShapeDtypeStruct((count,) + parts.shape[1:], jnp.float32),
        in_specs=[pl.BlockSpec(memory_space=pltpu.VMEM)],
        out_specs=pl.BlockSpec(memory_space=pltpu.VMEM),
        compiler_params=pltpu.CompilerParams(vmem_limit_bytes=SMALL_LIMIT),
        cost_estimate=pl.CostEstimate(flops=10**6, bytes_accessed=2 * 10**6, transcendentals=0),
        name="sum_rows",
    )(parts)


def weights_kernel(place, *refs):
    arrays, grads, out = refs[:-2], refs[-2], refs[-1]
    count = grads.shape[0] // 2
    rows = out.shape[1]
    slots = out.shape[0] // 2
    sources = [lax.rem(place[0] - back + count, count) * 2 for back in range(count)]
    here, there = place[2], 1 - place[2]
    right = jnp.concatenate([grads[s + here] for s in sources] + [grads[s + there] for s in sources], axis=0)
    slabs = [(ref, i) for ref in arrays for i in range(ref.shape[0])]
    each = len(slabs) // 2
    for high in range(2):
        blocks = [ref[i] for ref, i in slabs[high * each:(high + 1) * each]]
        result = nn(jnp.concatenate(blocks, axis=1), right).astype(jnp.bfloat16)
        block = lax.bitwise_xor(place[1], high)
        for slot in range(slots):
            out[block * slots + slot] = result[slot * rows:(slot + 1) * rows]


def weights_call(place, arrays, grads, slots):
    rows = arrays[0].shape[1] // slots
    return pl.pallas_call(
        weights_kernel,
        out_shape=jax.ShapeDtypeStruct((2 * slots, rows, grads.shape[2]), jnp.bfloat16),
        in_specs=in_vmem(1 + len(arrays)),
        out_specs=pl.BlockSpec(memory_space=pltpu.VMEM),
        compiler_params=pltpu.CompilerParams(vmem_limit_bytes=SMALL_LIMIT),
        cost_estimate=pl.CostEstimate(flops=10**9, bytes_accessed=4 * 10**6, transcendentals=0),
        name="weights",
    )(place, *arrays, grads)


def around(array, axis, by):
    size = lax.axis_size(axis)
    return lax.ppermute(array, axis, [(i, (i + by) % size) for i in range(size)])


def swapped(array, axis):
    return lax.ppermute(array, axis, [(0, 1), (1, 0)])


def tables(doc_lengths, span_order):
    count = span_order.shape[0]
    outer, inner = lax.axis_size("ya"), lax.axis_size("z")
    side = lax.axis_index("yb")
    boundary = jnp.cumsum(doc_lengths[0])
    order = span_order.reshape(outer, 2, inner)
    mine = jnp.where(side == 0, order[:, 0], order[:, 1]).reshape(-1)
    spans = jnp.stack([mine, 2 * count - 1 - mine], axis=1).reshape(-1)
    rank = jnp.sum((spans[None, :] < spans[:, None]).astype(jnp.int32), axis=1)
    ctx = lax.axis_index(("ya", "yb", "z"))
    ids = jnp.arange(count, dtype=jnp.int32)
    first = jnp.sum(jnp.where(ids == ctx, span_order, 0))
    partner = ctx + (1 - 2 * side) * inner
    second = jnp.sum(jnp.where(ids == partner, span_order, 0))
    q_spans = jnp.stack([first, 2 * count - 1 - first, second, 2 * count - 1 - second])

    def doc_start(positions):
        reached = boundary <= positions[..., None]
        return jnp.max(jnp.where(reached, boundary, 0), axis=-1)

    low = doc_start(q_spans * SPAN) // SPAN
    lower = jnp.sum((spans[None, :] < low[:, None]).astype(jnp.int32), axis=1) // SPANS_PER_TILE
    upper = jnp.sum((spans[None, :] <= q_spans[:, None]).astype(jnp.int32), axis=1)
    upper = (upper + SPANS_PER_TILE - 1) // SPANS_PER_TILE
    bounds = jnp.concatenate([lower, upper, jnp.zeros((spans.shape[0] - 8,), jnp.int32)])
    meta = jnp.stack([rank, spans, bounds])
    return meta, q_spans, doc_start


def shards(queries, keys, values, out_grad, normed_input, doc_lengths, span_order):
    height = queries.shape[1]
    heads = queries.shape[2] // HEAD
    group = ("ya", "z")
    group_size = lax.axis_size("ya") * lax.axis_size("z")
    depth = lax.axis_size("z")

    def laid(array):
        return array.reshape(2, SPAN, heads, HEAD).transpose(0, 2, 1, 3).reshape(heads * height, HEAD)

    own = jnp.stack([laid(queries[0]), laid(out_grad[0])])
    other = swapped(own, "yb")
    pair = jnp.concatenate([keys[0], values[0]], axis=1)
    kv = lax.all_to_all(
        jnp.broadcast_to(pair[None], (group_size,) + pair.shape), group, 0, 0, tiled=True
    )

    meta, q_spans, doc_start = tables(doc_lengths, span_order)
    q_pos = q_spans[:, None] * SPAN + jnp.arange(SPAN, dtype=jnp.int32)[None, :]
    q_start = doc_start(q_pos)
    qmeta = jnp.pad(jnp.stack([q_pos, q_start], axis=1).reshape(8, SPAN), ((0, 8), (0, 0)), constant_values=-1)
    qmeta = jnp.tile(qmeta, (1, heads))

    other, features = lax.optimization_barrier((other, normed_input))
    copies_of = lax.axis_size("dp")
    replica = lax.axis_index("dp")
    rows = normed_input.shape[2] // (depth * copies_of)
    slabs = features[0].reshape(height, depth, copies_of, rows).transpose(2, 1, 3, 0)
    slabs = slabs.reshape(copies_of, depth * rows, height)
    columns = []
    for by in range(copies_of):
        place = lax.rem(replica + by, copies_of)
        slab = lax.dynamic_index_in_dim(slabs, place, 0, keepdims=False)
        columns.append(
            lax.ppermute(
                slab,
                ("dp", "yb", "core"),
                [
                    (d * 4 + b * 2 + c, (d + by) % copies_of * 4 + c * 2 + b)
                    for d in range(copies_of) for b in range(2) for c in range(2)
                ],
            )
        )
    stats = stats_call(meta, qmeta, own, other, kv)
    stats, columns = lax.optimization_barrier((stats, columns))
    far = swapped(stats, "yb")
    far, near = lax.optimization_barrier((far, jnp.stack(columns)))
    dq_own, dq_other, dkv = grad_call(meta, qmeta, own, other, kv, stats, far)

    place = jnp.stack(
        [replica, lax.axis_index("yh"), lax.axis_index("core"), lax.axis_index("ya")]
    ).astype(jnp.int32)
    dkv, late = lax.optimization_barrier((dkv, near))
    beside = swapped(late, "yh")
    parts = lax.all_to_all(dkv, "z", 0, 0, tiled=True)
    halves = late[:copies_of // 2], late[copies_of // 2:]
    near_across = [swapped(part, "core") for part in halves]
    parts, beside, near_across = lax.optimization_barrier((parts, beside, near_across))
    kept, sent_grads = first_sum(place, parts)
    got = swapped(sent_grads, "ya")
    dq_far = swapped(dq_other, "yb")
    got, beside = lax.optimization_barrier((got, beside))
    beside_across = swapped(beside, "core")
    copies, key_grad, value_grad = second_sum(kept, got, 2 * copies_of)

    all_grads = lax.all_to_all(copies, ("dp", "yb"), 0, 0, tiled=True)
    blocks = weights_call(place, (late, *near_across, beside, beside_across), all_grads, depth)
    pieces = lax.all_to_all(blocks, group, 0, 0, tiled=True)
    spread = sum_rows(pieces, copies_of)
    weight = lax.all_to_all(spread, "dp", 0, 0, tiled=True).reshape(copies_of * rows, 2 * HEAD)
    query_grad = (dq_own + dq_far.astype(jnp.float32)).astype(jnp.bfloat16)[None]
    return (query_grad, key_grad[None], value_grad[None], weight[:, :HEAD], weight[:, HEAD:])


def solution(mesh):
    sizes = dict(mesh.shape)
    deep = sizes["ctx"] // 4
    fine = Mesh(
        mesh.devices.reshape(sizes["dp"], 2, 2, deep, 2, sizes["tp"] // 2),
        ("dp", "ya", "yb", "z", "yh", "core"),
    )
    context, model = ("ya", "yb", "z"), ("yh", "core")
    in_specs = (
        P("dp", context, model),
        P("dp", context, model),
        P("dp", context, model),
        P("dp", context, model),
        P("dp", context, model),
        P("dp", None),
        P(),
    )
    out_specs = (
        P("dp", context, model),
        P("dp", context, model),
        P("dp", context, model),
        P(context, model),
        P(context, model),
    )
    return jax.shard_map(shards, mesh=fine, in_specs=in_specs, out_specs=out_specs, check_vma=False)
```

```python
import jax
import jax.numpy as jnp
from jax import lax
from jax.experimental import pallas as pl
from jax.experimental.pallas import tpu as pltpu
from jax.sharding import Mesh, PartitionSpec as P

HEAD = 128
SPAN = 64
TILE = 256
SPANS_PER_TILE = TILE // SPAN
NEG = -1e30
SCALE = HEAD ** (-0.5)
LOG2E = 1.4426950408889634
VMEM_LIMIT = 24 * 1024 * 1024
SMALL_LIMIT = 12 * 1024 * 1024


def nt(left, right):
    return lax.dot_general(left, right, (((1,), (1,)), ((), ())), preferred_element_type=jnp.float32)


def tn(left, right):
    return lax.dot_general(left, right, (((0,), (0,)), ((), ())), preferred_element_type=jnp.float32)


def nn(left, right):
    return lax.dot_general(left, right, (((1,), (0,)), ((), ())), preferred_element_type=jnp.float32)


def load_operands(meta, own, other, kv, q_s, g_s, k_s, v_s, pos_s):
    rows = own.shape[1]
    for source, block in enumerate((own, other)):
        q_s[source * rows:(source + 1) * rows, :] = block[0]
        g_s[source * rows:(source + 1) * rows, :] = block[1]
    lane_rows = lax.broadcasted_iota(jnp.int32, (SPAN, 128), 0)

    def place(block, carry):
        for half in range(2):
            span = 2 * block + half
            start = pl.multiple_of(meta[0, span] * SPAN, SPAN)
            piece = kv[block, half * SPAN:(half + 1) * SPAN, :]
            k_s[pl.ds(start, SPAN), :] = piece[:, :HEAD]
            v_s[pl.ds(start, SPAN), :] = piece[:, HEAD:]
            pos_s[pl.ds(start, SPAN), :] = lane_rows + meta[1, span] * SPAN
        return carry

    lax.fori_loop(0, kv.shape[0], place, 0, unroll=True)


def masked_scores(k_tile, q_rows, pos_tile, q_pos, q_start):
    copies = q_rows.shape[0] // 128
    key_pos = jnp.concatenate([pos_tile] * copies, axis=1)
    mask = (key_pos - q_start).astype(jnp.uint32) <= (q_pos - q_start).astype(jnp.uint32)
    return jnp.where(mask, nt(k_tile, q_rows) * (SCALE * LOG2E), NEG)


def list_tiles(meta, items, together):
    def add(t, n, u):
        items[n] = u * 32 + t
        return n + 1

    count = jnp.int32(0)
    for u in range(4):
        count = lax.fori_loop(meta[2, u], meta[2, 4 + u], lambda t, n, u=u: add(t, n, u), count)
    for spare in range(together - 1):
        items[count + spare] = 4 * 32
    return lax.div(count + together - 1, together)


def tile_scores(item, qmeta, q_s, k_s, pos_s):
    u, t = lax.shift_right_logical(item, 5), item & 31
    here = pl.ds(pl.multiple_of(t * TILE, TILE), TILE)
    span = lax.rem(u, 4)
    rows = qmeta.shape[1]
    base = pl.ds(pl.multiple_of(span * rows, rows), rows)
    scores = masked_scores(
        k_s[here, :], q_s[base, :], pos_s[here, :], qmeta[pl.ds(2 * u, 1), :], qmeta[pl.ds(2 * u + 1, 1), :]
    )
    return span, base, here, t, scores


def stats_kernel(meta, qmeta, own, other, kv, out, q_s, g_s, k_s, v_s, pos_s, items):
    load_operands(meta, own, other, kv, q_s, g_s, k_s, v_s, pos_s)
    rows = qmeta.shape[1]
    out[0:4, :] = jnp.full((4, rows), NEG, jnp.float32)
    out[4:16, :] = jnp.zeros((12, rows), jnp.float32)
    groups = list_tiles(meta, items, 2)

    def group_step(group, carry):
        found = []
        for slot in range(2):
            span, base, here, t, scores = tile_scores(items[group * 2 + slot], qmeta, q_s, k_s, pos_s)
            top = jnp.max(scores, axis=0, keepdims=True)
            probs = jnp.exp2(scores - top)
            grad = nt(v_s[here, :], g_s[base, :])
            total = jnp.sum(probs, axis=0, keepdims=True)
            found.append((span, top, total, jnp.sum(probs * grad, axis=0, keepdims=True)))
        for span, top, total, weighted in found:
            before = out[pl.ds(span, 1), :]
            new_top = jnp.maximum(before, top)
            keep, scale = jnp.exp2(before - new_top), jnp.exp2(top - new_top)
            out[pl.ds(span, 1), :] = new_top
            out[pl.ds(4 + span, 1), :] = keep * out[pl.ds(4 + span, 1), :] + scale * total
            out[pl.ds(8 + span, 1), :] = keep * out[pl.ds(8 + span, 1), :] + scale * weighted
        return carry

    lax.fori_loop(0, groups, group_step, 0)


def grad_kernel(
    meta, qmeta, own, other, kv, stats, far, dq_own, dq_other, dkv,
    q_s, g_s, k_s, v_s, pos_s, items, dk_s, dv_s, dq_s, fin_s,
):
    load_operands(meta, own, other, kv, q_s, g_s, k_s, v_s, pos_s)
    rows = qmeta.shape[1]
    heads = rows // SPAN
    dk_s[...] = jnp.zeros_like(dk_s)
    dv_s[...] = jnp.zeros_like(dv_s)
    dq_s[...] = jnp.zeros_like(dq_s)
    for u in range(4):
        v = (u + 2) % 4
        top_a, top_b = stats[u:u + 1, :], far[v:v + 1, :]
        top = jnp.maximum(top_a, top_b)
        scale_a, scale_b = jnp.exp2(top_a - top), jnp.exp2(top_b - top)
        total = scale_a * stats[4 + u:5 + u, :] + scale_b * far[4 + v:5 + v, :]
        weighted = scale_a * stats[8 + u:9 + u, :] + scale_b * far[8 + v:9 + v, :]
        fin_s[u:u + 1, :] = top + jnp.log(total) * LOG2E
        fin_s[4 + u:5 + u, :] = weighted / total
    groups = list_tiles(meta, items, 2)

    def group_step(group, carry):
        found = []
        for slot in range(2):
            span, base, here, t, scores = tile_scores(items[group * 2 + slot], qmeta, q_s, k_s, pos_s)
            probs = jnp.exp2(scores - fin_s[pl.ds(span, 1), :])
            grad = nt(v_s[here, :], g_s[base, :])
            score_grad = (probs * (grad - fin_s[pl.ds(4 + span, 1), :])).astype(jnp.bfloat16)
            found.append((
                span, here, nn(probs.astype(jnp.bfloat16), g_s[base, :]), nn(score_grad, q_s[base, :]),
                tn(k_s[here, :], score_grad),
            ))
        for span, here, value_part, key_part, query_part in found:
            dv_s[here, :] += value_part
            dk_s[here, :] += key_part
            dq_s[span] += query_part
        return carry

    lax.fori_loop(0, groups, group_step, 0)
    for u in range(4):
        flat = (dq_s[u] * SCALE).T
        half = (u % 2) * SPAN
        for head in range(heads):
            piece = flat[head * SPAN:(head + 1) * SPAN, :]
            if u < 2:
                dq_own[half:half + SPAN, head * HEAD:(head + 1) * HEAD] = piece
            else:
                dq_other[half:half + SPAN, head * HEAD:(head + 1) * HEAD] = piece.astype(jnp.bfloat16)

    depth = dkv.shape[0] // 2

    def unplace(block, carry):
        for half in range(2):
            start = pl.multiple_of(meta[0, 2 * block + half] * SPAN, SPAN)
            here = pl.ds(start, SPAN)
            there = lax.rem(block, depth) * 2 + lax.div(block, depth)
            dkv[there, half * SPAN:(half + 1) * SPAN, :HEAD] = (dk_s[here, :] * SCALE).astype(jnp.bfloat16)
            dkv[there, half * SPAN:(half + 1) * SPAN, HEAD:] = dv_s[here, :].astype(jnp.bfloat16)
        return carry

    lax.fori_loop(0, dkv.shape[0], unplace, 0, unroll=True)


def operand_scratch(rows, keys):
    return [
        pltpu.VMEM((4 * rows, HEAD), jnp.bfloat16),
        pltpu.VMEM((4 * rows, HEAD), jnp.bfloat16),
        pltpu.VMEM((keys, HEAD), jnp.bfloat16),
        pltpu.VMEM((keys, HEAD), jnp.bfloat16),
        pltpu.VMEM((keys, 128), jnp.int32),
        pltpu.SMEM((4 * (keys // TILE) + 8,), jnp.int32),
    ]


def in_vmem(count):
    return [pl.BlockSpec(memory_space=pltpu.SMEM)] + [pl.BlockSpec(memory_space=pltpu.VMEM)] * count


def stats_call(meta, qmeta, own, other, kv):
    rows = qmeta.shape[1]
    keys = kv.shape[0] * kv.shape[1]
    return pl.pallas_call(
        stats_kernel,
        out_shape=jax.ShapeDtypeStruct((16, rows), jnp.float32),
        in_specs=in_vmem(4),
        out_specs=pl.BlockSpec(memory_space=pltpu.VMEM),
        scratch_shapes=operand_scratch(rows, keys),
        compiler_params=pltpu.CompilerParams(vmem_limit_bytes=VMEM_LIMIT),
        cost_estimate=pl.CostEstimate(flops=2 * 10**9, bytes_accessed=4 * 10**6, transcendentals=10**6),
        name="stats",
    )(meta, qmeta, own, other, kv)


def grad_call(meta, qmeta, own, other, kv, stats, far):
    rows = qmeta.shape[1]
    keys = kv.shape[0] * kv.shape[1]
    height, width = 2 * SPAN, rows // SPAN * HEAD
    return pl.pallas_call(
        grad_kernel,
        out_shape=(
            jax.ShapeDtypeStruct((height, width), jnp.float32),
            jax.ShapeDtypeStruct((height, width), jnp.bfloat16),
            jax.ShapeDtypeStruct(kv.shape, jnp.bfloat16),
        ),
        in_specs=in_vmem(6),
        out_specs=[pl.BlockSpec(memory_space=pltpu.VMEM)] * 3,
        scratch_shapes=operand_scratch(rows, keys) + [
            pltpu.VMEM((keys, HEAD), jnp.float32),
            pltpu.VMEM((keys, HEAD), jnp.float32),
            pltpu.VMEM((4, HEAD, rows), jnp.float32),
            pltpu.VMEM((8, rows), jnp.float32),
        ],
        compiler_params=pltpu.CompilerParams(vmem_limit_bytes=VMEM_LIMIT),
        cost_estimate=pl.CostEstimate(flops=5 * 10**9, bytes_accessed=6 * 10**6, transcendentals=10**6),
        name="grads",
    )(meta, qmeta, own, other, kv, stats, far)


def first_sum_kernel(place, parts, kept, sent):
    for where, out in ((place[3], kept), (1 - place[3], sent)):
        total = parts[where].astype(jnp.float32)
        for level in range(1, parts.shape[0] // 2):
            total += parts[2 * level + where].astype(jnp.float32)
        out[...] = total.astype(out.dtype)


def first_sum(place, parts):
    shape = parts.shape[1:]
    return pl.pallas_call(
        first_sum_kernel,
        out_shape=[jax.ShapeDtypeStruct(shape, jnp.float32), jax.ShapeDtypeStruct(shape, jnp.bfloat16)],
        in_specs=in_vmem(1),
        out_specs=[pl.BlockSpec(memory_space=pltpu.VMEM)] * 2,
        compiler_params=pltpu.CompilerParams(vmem_limit_bytes=SMALL_LIMIT),
        cost_estimate=pl.CostEstimate(flops=10**6, bytes_accessed=2 * 10**6, transcendentals=0),
        name="first_sum",
    )(place, parts)


def second_sum_kernel(kept, got, copies, key_out, value_out):
    rounded = (kept[...] + got[...].astype(jnp.float32)).astype(jnp.bfloat16)
    for copy in range(copies.shape[0]):
        copies[copy] = rounded
    key_out[...] = rounded[:, :HEAD]
    value_out[...] = rounded[:, HEAD:]


def second_sum(kept, got, count):
    height, width = kept.shape
    half = jax.ShapeDtypeStruct((height, HEAD), jnp.bfloat16)
    return pl.pallas_call(
        second_sum_kernel,
        out_shape=[jax.ShapeDtypeStruct((count, height, width), jnp.bfloat16), half, half],
        in_specs=[pl.BlockSpec(memory_space=pltpu.VMEM)] * 2,
        out_specs=[pl.BlockSpec(memory_space=pltpu.VMEM)] * 3,
        compiler_params=pltpu.CompilerParams(vmem_limit_bytes=SMALL_LIMIT),
        cost_estimate=pl.CostEstimate(flops=10**6, bytes_accessed=10**6, transcendentals=0),
        name="second_sum",
    )(kept, got)


def sum_rows_kernel(parts, copies):
    total = parts[0].astype(jnp.float32)
    for part in range(1, parts.shape[0]):
        total += parts[part].astype(jnp.float32)
    for copy in range(copies.shape[0]):
        copies[copy] = total


def sum_rows(parts, count):
    return pl.pallas_call(
        sum_rows_kernel,
        out_shape=jax.ShapeDtypeStruct((count,) + parts.shape[1:], jnp.float32),
        in_specs=[pl.BlockSpec(memory_space=pltpu.VMEM)],
        out_specs=pl.BlockSpec(memory_space=pltpu.VMEM),
        compiler_params=pltpu.CompilerParams(vmem_limit_bytes=SMALL_LIMIT),
        cost_estimate=pl.CostEstimate(flops=10**6, bytes_accessed=2 * 10**6, transcendentals=0),
        name="sum_rows",
    )(parts)


def weights_kernel(place, *refs):
    arrays, grads, out = refs[:-2], refs[-2], refs[-1]
    count = grads.shape[0] // 2
    rows = out.shape[1]
    slots = out.shape[0] // 2
    sources = [lax.rem(place[0] - back + count, count) * 2 for back in range(count)]
    here, there = place[2], 1 - place[2]
    right = jnp.concatenate([grads[s + here] for s in sources] + [grads[s + there] for s in sources], axis=0)
    slabs = [(ref, i) for ref in arrays for i in range(ref.shape[0])]
    each = len(slabs) // 2
    for high in range(2):
        blocks = [ref[i] for ref, i in slabs[high * each:(high + 1) * each]]
        result = nn(jnp.concatenate(blocks, axis=1), right).astype(jnp.bfloat16)
        block = lax.bitwise_xor(place[1], high)
        for slot in range(slots):
            out[block * slots + slot] = result[slot * rows:(slot + 1) * rows]


def weights_call(place, arrays, grads, slots):
    rows = arrays[0].shape[1] // slots
    return pl.pallas_call(
        weights_kernel,
        out_shape=jax.ShapeDtypeStruct((2 * slots, rows, grads.shape[2]), jnp.bfloat16),
        in_specs=in_vmem(1 + len(arrays)),
        out_specs=pl.BlockSpec(memory_space=pltpu.VMEM),
        compiler_params=pltpu.CompilerParams(vmem_limit_bytes=SMALL_LIMIT),
        cost_estimate=pl.CostEstimate(flops=10**9, bytes_accessed=4 * 10**6, transcendentals=0),
        name="weights",
    )(place, *arrays, grads)


def swapped(array, axis):
    return lax.ppermute(array, axis, [(0, 1), (1, 0)])


def tables(doc_lengths, span_order):
    count = span_order.shape[0]
    outer, inner = lax.axis_size("ya"), lax.axis_size("z")
    side = lax.axis_index("yb")
    boundary = jnp.cumsum(doc_lengths[0])
    order = span_order.reshape(outer, 2, inner)
    mine = jnp.where(side == 0, order[:, 0], order[:, 1]).reshape(-1)
    spans = jnp.stack([mine, 2 * count - 1 - mine], axis=1).reshape(-1)
    rank = jnp.sum((spans[None, :] < spans[:, None]).astype(jnp.int32), axis=1)
    ctx = lax.axis_index(("ya", "yb", "z"))
    ids = jnp.arange(count, dtype=jnp.int32)
    first = jnp.sum(jnp.where(ids == ctx, span_order, 0))
    partner = ctx + (1 - 2 * side) * inner
    second = jnp.sum(jnp.where(ids == partner, span_order, 0))
    q_spans = jnp.stack([first, 2 * count - 1 - first, second, 2 * count - 1 - second])

    def doc_start(positions):
        reached = boundary <= positions[..., None]
        return jnp.max(jnp.where(reached, boundary, 0), axis=-1)

    low = doc_start(q_spans * SPAN) // SPAN
    lower = jnp.sum((spans[None, :] < low[:, None]).astype(jnp.int32), axis=1) // SPANS_PER_TILE
    upper = jnp.sum((spans[None, :] <= q_spans[:, None]).astype(jnp.int32), axis=1)
    upper = (upper + SPANS_PER_TILE - 1) // SPANS_PER_TILE
    bounds = jnp.concatenate([lower, upper, jnp.zeros((spans.shape[0] - 8,), jnp.int32)])
    meta = jnp.stack([rank, spans, bounds])
    return meta, q_spans, doc_start


def shards(queries, keys, values, out_grad, normed_input, doc_lengths, span_order):
    height = queries.shape[1]
    heads = queries.shape[2] // HEAD
    group = ("ya", "z")
    group_size = lax.axis_size("ya") * lax.axis_size("z")
    depth = lax.axis_size("z")

    def laid(array):
        return array.reshape(2, SPAN, heads, HEAD).transpose(0, 2, 1, 3).reshape(heads * height, HEAD)

    own = jnp.stack([laid(queries[0]), laid(out_grad[0])])
    other = swapped(own, "yb")
    pair = jnp.concatenate([keys[0], values[0]], axis=1)
    kv = lax.all_to_all(
        jnp.broadcast_to(pair[None], (group_size,) + pair.shape), group, 0, 0, tiled=True
    )

    meta, q_spans, doc_start = tables(doc_lengths, span_order)
    q_pos = q_spans[:, None] * SPAN + jnp.arange(SPAN, dtype=jnp.int32)[None, :]
    q_start = doc_start(q_pos)
    qmeta = jnp.pad(jnp.stack([q_pos, q_start], axis=1).reshape(8, SPAN), ((0, 8), (0, 0)), constant_values=-1)
    qmeta = jnp.tile(qmeta, (1, heads))

    other, features = lax.optimization_barrier((other, normed_input))
    copies_of = lax.axis_size("dp")
    replica = lax.axis_index("dp")
    rows = normed_input.shape[2] // (depth * copies_of)
    slabs = features[0].reshape(height, depth, copies_of, rows).transpose(2, 1, 3, 0)
    slabs = slabs.reshape(copies_of, depth * rows, height)
    columns = []
    for by in range(copies_of):
        place = lax.rem(replica + by, copies_of)
        slab = lax.dynamic_index_in_dim(slabs, place, 0, keepdims=False)
        columns.append(
            lax.ppermute(
                slab,
                ("dp", "yb", "core"),
                [
                    (d * 4 + b * 2 + c, (d + by) % copies_of * 4 + c * 2 + b)
                    for d in range(copies_of) for b in range(2) for c in range(2)
                ],
            )
        )
    stats = stats_call(meta, qmeta, own, other, kv)
    stats, columns = lax.optimization_barrier((stats, columns))
    far = swapped(stats, "yb")
    far, near = lax.optimization_barrier((far, jnp.stack(columns)))
    dq_own, dq_other, dkv = grad_call(meta, qmeta, own, other, kv, stats, far)

    place = jnp.stack(
        [replica, lax.axis_index("yh"), lax.axis_index("core"), lax.axis_index("ya")]
    ).astype(jnp.int32)
    dkv, late = lax.optimization_barrier((dkv, near))
    beside = swapped(late, "yh")
    parts = lax.all_to_all(dkv, "z", 0, 0, tiled=True)
    halves = late[:copies_of // 2], late[copies_of // 2:]
    near_across = [swapped(part, "core") for part in halves]
    parts, beside, near_across = lax.optimization_barrier((parts, beside, near_across))
    kept, sent_grads = first_sum(place, parts)
    got = swapped(sent_grads, "ya")
    dq_far = swapped(dq_other, "yb")
    got, beside = lax.optimization_barrier((got, beside))
    beside_across = swapped(beside, "core")
    copies, key_grad, value_grad = second_sum(kept, got, 2 * copies_of)

    all_grads = lax.all_to_all(copies, ("dp", "yb"), 0, 0, tiled=True)
    blocks = weights_call(place, (late, *near_across, beside, beside_across), all_grads, depth)
    pieces = lax.all_to_all(blocks, group, 0, 0, tiled=True)
    spread = sum_rows(pieces, copies_of)
    weight = lax.all_to_all(spread, "dp", 0, 0, tiled=True).reshape(copies_of * rows, 2 * HEAD)
    query_grad = (dq_own + dq_far.astype(jnp.float32)).astype(jnp.bfloat16)[None]
    return (query_grad, key_grad[None], value_grad[None], weight[:, :HEAD], weight[:, HEAD:])


def solution(mesh):
    sizes = dict(mesh.shape)
    deep = sizes["ctx"] // 4
    fine = Mesh(
        mesh.devices.reshape(sizes["dp"], 2, 2, deep, 2, sizes["tp"] // 2),
        ("dp", "ya", "yb", "z", "yh", "core"),
    )
    context, model = ("ya", "yb", "z"), ("yh", "core")
    in_specs = (
        P("dp", context, model),
        P("dp", context, model),
        P("dp", context, model),
        P("dp", context, model),
        P("dp", context, model),
        P("dp", None),
        P(),
    )
    out_specs = (
        P("dp", context, model),
        P("dp", context, model),
        P("dp", context, model),
        P(context, model),
        P(context, model),
    )
    return jax.shard_map(shards, mesh=fine, in_specs=in_specs, out_specs=out_specs, check_vma=False)
```

```python
import jax
import jax.numpy as jnp
from jax import lax
from jax.experimental import pallas as pl
from jax.experimental.pallas import tpu as pltpu
from jax.sharding import Mesh, PartitionSpec as P

HEAD = 128
SPAN = 64
TILE = 256
SPANS_PER_TILE = TILE // SPAN
NEG = -1e30
SCALE = HEAD ** (-0.5)
LOG2E = 1.4426950408889634
VMEM_LIMIT = 24 * 1024 * 1024
SMALL_LIMIT = 12 * 1024 * 1024


def nt(left, right):
    return lax.dot_general(left, right, (((1,), (1,)), ((), ())), preferred_element_type=jnp.float32)


def tn(left, right):
    return lax.dot_general(left, right, (((0,), (0,)), ((), ())), preferred_element_type=jnp.float32)


def nn(left, right):
    return lax.dot_general(left, right, (((1,), (0,)), ((), ())), preferred_element_type=jnp.float32)


def load_operands(meta, own, other, kv, q_s, g_s, k_s, v_s, pos_s):
    rows = own.shape[1]
    for source, block in enumerate((own, other)):
        q_s[source * rows:(source + 1) * rows, :] = block[0]
        g_s[source * rows:(source + 1) * rows, :] = block[1]
    lane_rows = lax.broadcasted_iota(jnp.int32, (SPAN, 128), 0)

    def place(block, carry):
        for half in range(2):
            span = 2 * block + half
            start = pl.multiple_of(meta[0, span] * SPAN, SPAN)
            piece = kv[block, half * SPAN:(half + 1) * SPAN, :]
            k_s[pl.ds(start, SPAN), :] = piece[:, :HEAD]
            v_s[pl.ds(start, SPAN), :] = piece[:, HEAD:]
            pos_s[pl.ds(start, SPAN), :] = lane_rows + meta[1, span] * SPAN
        return carry

    lax.fori_loop(0, kv.shape[0], place, 0, unroll=True)


def masked_scores(k_tile, q_rows, pos_tile, q_pos, q_start):
    copies = q_rows.shape[0] // 128
    key_pos = jnp.concatenate([pos_tile] * copies, axis=1)
    mask = (key_pos - q_start).astype(jnp.uint32) <= (q_pos - q_start).astype(jnp.uint32)
    return jnp.where(mask, nt(k_tile, q_rows) * (SCALE * LOG2E), NEG)


def list_tiles(meta, items, together):
    def add(t, n, u):
        items[n] = u * 32 + t
        return n + 1

    count = jnp.int32(0)
    for u in range(4):
        count = lax.fori_loop(meta[2, u], meta[2, 4 + u], lambda t, n, u=u: add(t, n, u), count)
    for spare in range(together - 1):
        items[count + spare] = 4 * 32
    return lax.div(count + together - 1, together)


def tile_scores(item, qmeta, q_s, k_s, pos_s):
    u, t = lax.shift_right_logical(item, 5), item & 31
    here = pl.ds(pl.multiple_of(t * TILE, TILE), TILE)
    span = lax.rem(u, 4)
    rows = qmeta.shape[1]
    base = pl.ds(pl.multiple_of(span * rows, rows), rows)
    scores = masked_scores(
        k_s[here, :], q_s[base, :], pos_s[here, :], qmeta[pl.ds(2 * u, 1), :], qmeta[pl.ds(2 * u + 1, 1), :]
    )
    return span, base, here, t, scores


def stats_kernel(meta, qmeta, own, other, kv, out, q_s, g_s, k_s, v_s, pos_s, items):
    load_operands(meta, own, other, kv, q_s, g_s, k_s, v_s, pos_s)
    rows = qmeta.shape[1]
    out[0:4, :] = jnp.full((4, rows), NEG, jnp.float32)
    out[4:16, :] = jnp.zeros((12, rows), jnp.float32)
    groups = list_tiles(meta, items, 2)

    def group_step(group, carry):
        found = []
        for slot in range(2):
            span, base, here, t, scores = tile_scores(items[group * 2 + slot], qmeta, q_s, k_s, pos_s)
            top = jnp.max(scores, axis=0, keepdims=True)
            probs = jnp.exp2(scores - top)
            grad = nt(v_s[here, :], g_s[base, :])
            total = jnp.sum(probs, axis=0, keepdims=True)
            found.append((span, top, total, jnp.sum(probs * grad, axis=0, keepdims=True)))
        for span, top, total, weighted in found:
            before = out[pl.ds(span, 1), :]
            new_top = jnp.maximum(before, top)
            keep, scale = jnp.exp2(before - new_top), jnp.exp2(top - new_top)
            out[pl.ds(span, 1), :] = new_top
            out[pl.ds(4 + span, 1), :] = keep * out[pl.ds(4 + span, 1), :] + scale * total
            out[pl.ds(8 + span, 1), :] = keep * out[pl.ds(8 + span, 1), :] + scale * weighted
        return carry

    lax.fori_loop(0, groups, group_step, 0)


def grad_kernel(
    meta, qmeta, own, other, kv, stats, far, dq_own, dq_other, dkv,
    q_s, g_s, k_s, v_s, pos_s, items, dk_s, dv_s, dq_s, fin_s,
):
    load_operands(meta, own, other, kv, q_s, g_s, k_s, v_s, pos_s)
    rows = qmeta.shape[1]
    heads = rows // SPAN
    dk_s[...] = jnp.zeros_like(dk_s)
    dv_s[...] = jnp.zeros_like(dv_s)
    dq_s[...] = jnp.zeros_like(dq_s)
    for u in range(4):
        v = (u + 2) % 4
        top_a, top_b = stats[u:u + 1, :], far[v:v + 1, :]
        top = jnp.maximum(top_a, top_b)
        scale_a, scale_b = jnp.exp2(top_a - top), jnp.exp2(top_b - top)
        total = scale_a * stats[4 + u:5 + u, :] + scale_b * far[4 + v:5 + v, :]
        weighted = scale_a * stats[8 + u:9 + u, :] + scale_b * far[8 + v:9 + v, :]
        fin_s[u:u + 1, :] = top + jnp.log(total) * LOG2E
        fin_s[4 + u:5 + u, :] = weighted / total
    groups = list_tiles(meta, items, 2)

    def group_step(group, carry):
        found = []
        for slot in range(2):
            span, base, here, t, scores = tile_scores(items[group * 2 + slot], qmeta, q_s, k_s, pos_s)
            probs = jnp.exp2(scores - fin_s[pl.ds(span, 1), :])
            grad = nt(v_s[here, :], g_s[base, :])
            score_grad = (probs * (grad - fin_s[pl.ds(4 + span, 1), :])).astype(jnp.bfloat16)
            found.append((
                span, here, nn(probs.astype(jnp.bfloat16), g_s[base, :]), nn(score_grad, q_s[base, :]),
                tn(k_s[here, :], score_grad),
            ))
        for span, here, value_part, key_part, query_part in found:
            dv_s[here, :] += value_part
            dk_s[here, :] += key_part
            dq_s[span] += query_part
        return carry

    lax.fori_loop(0, groups, group_step, 0)
    for u in range(4):
        flat = (dq_s[u] * SCALE).T
        half = (u % 2) * SPAN
        for head in range(heads):
            piece = flat[head * SPAN:(head + 1) * SPAN, :]
            if u < 2:
                dq_own[half:half + SPAN, head * HEAD:(head + 1) * HEAD] = piece
            else:
                dq_other[half:half + SPAN, head * HEAD:(head + 1) * HEAD] = piece.astype(jnp.bfloat16)

    depth = dkv.shape[0] // 2

    def unplace(block, carry):
        for half in range(2):
            start = pl.multiple_of(meta[0, 2 * block + half] * SPAN, SPAN)
            here = pl.ds(start, SPAN)
            there = lax.rem(block, depth) * 2 + lax.div(block, depth)
            dkv[there, half * SPAN:(half + 1) * SPAN, :HEAD] = (dk_s[here, :] * SCALE).astype(jnp.bfloat16)
            dkv[there, half * SPAN:(half + 1) * SPAN, HEAD:] = dv_s[here, :].astype(jnp.bfloat16)
        return carry

    lax.fori_loop(0, dkv.shape[0], unplace, 0, unroll=True)


def operand_scratch(rows, keys):
    return [
        pltpu.VMEM((4 * rows, HEAD), jnp.bfloat16),
        pltpu.VMEM((4 * rows, HEAD), jnp.bfloat16),
        pltpu.VMEM((keys, HEAD), jnp.bfloat16),
        pltpu.VMEM((keys, HEAD), jnp.bfloat16),
        pltpu.VMEM((keys, 128), jnp.int32),
        pltpu.SMEM((4 * (keys // TILE) + 8,), jnp.int32),
    ]


def in_vmem(count):
    return [pl.BlockSpec(memory_space=pltpu.SMEM)] + [pl.BlockSpec(memory_space=pltpu.VMEM)] * count


def stats_call(meta, qmeta, own, other, kv):
    rows = qmeta.shape[1]
    keys = kv.shape[0] * kv.shape[1]
    return pl.pallas_call(
        stats_kernel,
        out_shape=jax.ShapeDtypeStruct((16, rows), jnp.float32),
        in_specs=in_vmem(4),
        out_specs=pl.BlockSpec(memory_space=pltpu.VMEM),
        scratch_shapes=operand_scratch(rows, keys),
        compiler_params=pltpu.CompilerParams(vmem_limit_bytes=VMEM_LIMIT),
        cost_estimate=pl.CostEstimate(flops=2 * 10**9, bytes_accessed=4 * 10**6, transcendentals=10**6),
        name="stats",
    )(meta, qmeta, own, other, kv)


def grad_call(meta, qmeta, own, other, kv, stats, far):
    rows = qmeta.shape[1]
    keys = kv.shape[0] * kv.shape[1]
    height, width = 2 * SPAN, rows // SPAN * HEAD
    return pl.pallas_call(
        grad_kernel,
        out_shape=(
            jax.ShapeDtypeStruct((height, width), jnp.float32),
            jax.ShapeDtypeStruct((height, width), jnp.bfloat16),
            jax.ShapeDtypeStruct(kv.shape, jnp.bfloat16),
        ),
        in_specs=in_vmem(6),
        out_specs=[pl.BlockSpec(memory_space=pltpu.VMEM)] * 3,
        scratch_shapes=operand_scratch(rows, keys) + [
            pltpu.VMEM((keys, HEAD), jnp.float32),
            pltpu.VMEM((keys, HEAD), jnp.float32),
            pltpu.VMEM((4, HEAD, rows), jnp.float32),
            pltpu.VMEM((8, rows), jnp.float32),
        ],
        compiler_params=pltpu.CompilerParams(vmem_limit_bytes=VMEM_LIMIT),
        cost_estimate=pl.CostEstimate(flops=5 * 10**9, bytes_accessed=6 * 10**6, transcendentals=10**6),
        name="grads",
    )(meta, qmeta, own, other, kv, stats, far)


def first_sum_kernel(place, parts, kept, sent):
    for where, out in ((place[3], kept), (1 - place[3], sent)):
        total = parts[where].astype(jnp.float32)
        for level in range(1, parts.shape[0] // 2):
            total += parts[2 * level + where].astype(jnp.float32)
        out[...] = total.astype(out.dtype)


def first_sum(place, parts):
    shape = parts.shape[1:]
    return pl.pallas_call(
        first_sum_kernel,
        out_shape=[jax.ShapeDtypeStruct(shape, jnp.float32), jax.ShapeDtypeStruct(shape, jnp.bfloat16)],
        in_specs=in_vmem(1),
        out_specs=[pl.BlockSpec(memory_space=pltpu.VMEM)] * 2,
        compiler_params=pltpu.CompilerParams(vmem_limit_bytes=SMALL_LIMIT),
        cost_estimate=pl.CostEstimate(flops=10**6, bytes_accessed=2 * 10**6, transcendentals=0),
        name="first_sum",
    )(place, parts)


def second_sum_kernel(kept, got, copies, key_out, value_out):
    rounded = (kept[...] + got[...].astype(jnp.float32)).astype(jnp.bfloat16)
    for copy in range(copies.shape[0]):
        copies[copy] = rounded
    key_out[...] = rounded[:, :HEAD]
    value_out[...] = rounded[:, HEAD:]


def second_sum(kept, got, count):
    height, width = kept.shape
    half = jax.ShapeDtypeStruct((height, HEAD), jnp.bfloat16)
    return pl.pallas_call(
        second_sum_kernel,
        out_shape=[jax.ShapeDtypeStruct((count, height, width), jnp.bfloat16), half, half],
        in_specs=[pl.BlockSpec(memory_space=pltpu.VMEM)] * 2,
        out_specs=[pl.BlockSpec(memory_space=pltpu.VMEM)] * 3,
        compiler_params=pltpu.CompilerParams(vmem_limit_bytes=SMALL_LIMIT),
        cost_estimate=pl.CostEstimate(flops=10**6, bytes_accessed=10**6, transcendentals=0),
        name="second_sum",
    )(kept, got)


def sum_rows_kernel(parts, copies):
    total = parts[0].astype(jnp.float32)
    for part in range(1, parts.shape[0]):
        total += parts[part].astype(jnp.float32)
    for copy in range(copies.shape[0]):
        copies[copy] = total


def sum_rows(parts, count):
    return pl.pallas_call(
        sum_rows_kernel,
        out_shape=jax.ShapeDtypeStruct((count,) + parts.shape[1:], jnp.float32),
        in_specs=[pl.BlockSpec(memory_space=pltpu.VMEM)],
        out_specs=pl.BlockSpec(memory_space=pltpu.VMEM),
        compiler_params=pltpu.CompilerParams(vmem_limit_bytes=SMALL_LIMIT),
        cost_estimate=pl.CostEstimate(flops=10**6, bytes_accessed=2 * 10**6, transcendentals=0),
        name="sum_rows",
    )(parts)


def weights_kernel(place, *refs):
    arrays, grads, out = refs[:-2], refs[-2], refs[-1]
    count = grads.shape[0] // 2
    rows = out.shape[1]
    slots = out.shape[0] // 2
    sources = [lax.rem(place[0] - back + count, count) * 2 for back in range(count)]
    here, there = place[2], 1 - place[2]
    right = jnp.concatenate([grads[s + here] for s in sources] + [grads[s + there] for s in sources], axis=0)
    slabs = [(ref, i) for ref in arrays for i in range(ref.shape[0])]
    each = len(slabs) // 2
    for high in range(2):
        blocks = [ref[i] for ref, i in slabs[high * each:(high + 1) * each]]
        result = nn(jnp.concatenate(blocks, axis=1), right).astype(jnp.bfloat16)
        block = lax.bitwise_xor(place[1], high)
        for slot in range(slots):
            out[block * slots + slot] = result[slot * rows:(slot + 1) * rows]


def weights_call(place, arrays, grads, slots):
    rows = arrays[0].shape[1] // slots
    return pl.pallas_call(
        weights_kernel,
        out_shape=jax.ShapeDtypeStruct((2 * slots, rows, grads.shape[2]), jnp.bfloat16),
        in_specs=in_vmem(1 + len(arrays)),
        out_specs=pl.BlockSpec(memory_space=pltpu.VMEM),
        compiler_params=pltpu.CompilerParams(vmem_limit_bytes=SMALL_LIMIT),
        cost_estimate=pl.CostEstimate(flops=10**9, bytes_accessed=4 * 10**6, transcendentals=0),
        name="weights",
    )(place, *arrays, grads)


def swapped(array, axis):
    return lax.ppermute(array, axis, [(0, 1), (1, 0)])


def tables(doc_lengths, span_order):
    count = span_order.shape[0]
    outer, inner = lax.axis_size("ya"), lax.axis_size("z")
    side = lax.axis_index("yb")
    boundary = jnp.cumsum(doc_lengths[0])
    order = span_order.reshape(outer, 2, inner)
    mine = jnp.where(side == 0, order[:, 0], order[:, 1]).reshape(-1)
    spans = jnp.stack([mine, 2 * count - 1 - mine], axis=1).reshape(-1)
    rank = jnp.sum((spans[None, :] < spans[:, None]).astype(jnp.int32), axis=1)
    ctx = lax.axis_index(("ya", "yb", "z"))
    ids = jnp.arange(count, dtype=jnp.int32)
    first = jnp.sum(jnp.where(ids == ctx, span_order, 0))
    partner = ctx + (1 - 2 * side) * inner
    second = jnp.sum(jnp.where(ids == partner, span_order, 0))
    q_spans = jnp.stack([first, 2 * count - 1 - first, second, 2 * count - 1 - second])

    def doc_start(positions):
        reached = boundary <= positions[..., None]
        return jnp.max(jnp.where(reached, boundary, 0), axis=-1)

    low = doc_start(q_spans * SPAN) // SPAN
    lower = jnp.sum((spans[None, :] < low[:, None]).astype(jnp.int32), axis=1) // SPANS_PER_TILE
    upper = jnp.sum((spans[None, :] <= q_spans[:, None]).astype(jnp.int32), axis=1)
    upper = (upper + SPANS_PER_TILE - 1) // SPANS_PER_TILE
    bounds = jnp.concatenate([lower, upper, jnp.zeros((spans.shape[0] - 8,), jnp.int32)])
    meta = jnp.stack([rank, spans, bounds])
    return meta, q_spans, doc_start


def shards(queries, keys, values, out_grad, normed_input, doc_lengths, span_order):
    height = queries.shape[1]
    heads = queries.shape[2] // HEAD
    group = ("ya", "z")
    group_size = lax.axis_size("ya") * lax.axis_size("z")
    depth = lax.axis_size("z")

    def laid(array):
        return array.reshape(2, SPAN, heads, HEAD).transpose(0, 2, 1, 3).reshape(heads * height, HEAD)

    own = jnp.stack([laid(queries[0]), laid(out_grad[0])])
    other = swapped(own, "yb")
    pair = jnp.concatenate([keys[0], values[0]], axis=1)
    kv = lax.all_to_all(
        jnp.broadcast_to(pair[None], (group_size,) + pair.shape), group, 0, 0, tiled=True
    )

    meta, q_spans, doc_start = tables(doc_lengths, span_order)
    q_pos = q_spans[:, None] * SPAN + jnp.arange(SPAN, dtype=jnp.int32)[None, :]
    q_start = doc_start(q_pos)
    qmeta = jnp.pad(jnp.stack([q_pos, q_start], axis=1).reshape(8, SPAN), ((0, 8), (0, 0)), constant_values=-1)
    qmeta = jnp.tile(qmeta, (1, heads))

    other, features = lax.optimization_barrier((other, normed_input))
    copies_of = lax.axis_size("dp")
    replica = lax.axis_index("dp")
    rows = normed_input.shape[2] // (depth * copies_of)
    slabs = features[0].reshape(height, depth, copies_of, rows).transpose(2, 1, 3, 0)
    slabs = slabs.reshape(copies_of, depth * rows, height)
    columns = []
    for by in range(copies_of):
        place = lax.rem(replica + by, copies_of)
        slab = lax.dynamic_index_in_dim(slabs, place, 0, keepdims=False)
        columns.append(
            lax.ppermute(
                slab,
                ("dp", "yb", "core"),
                [
                    (d * 4 + b * 2 + c, (d + by) % copies_of * 4 + c * 2 + b)
                    for d in range(copies_of) for b in range(2) for c in range(2)
                ],
            )
        )
    stats = stats_call(meta, qmeta, own, other, kv)
    stats, columns = lax.optimization_barrier((stats, columns))
    far = swapped(stats, "yb")
    far, near = lax.optimization_barrier((far, jnp.stack(columns)))
    dq_own, dq_other, dkv = grad_call(meta, qmeta, own, other, kv, stats, far)

    place = jnp.stack(
        [replica, lax.axis_index("yh"), lax.axis_index("core"), lax.axis_index("ya")]
    ).astype(jnp.int32)
    dkv, late = lax.optimization_barrier((dkv, near))
    beside = swapped(late, "yh")
    parts = lax.all_to_all(dkv, "z", 0, 0, tiled=True)
    halves = late[:copies_of // 2], late[copies_of // 2:]
    near_across = [swapped(part, "core") for part in halves]
    parts, near_across = lax.optimization_barrier((parts, near_across))
    kept, sent_grads = first_sum(place, parts)
    got = swapped(sent_grads, "ya")
    dq_far = swapped(dq_other, "yb")
    got, beside = lax.optimization_barrier((got, beside))
    beside_across = swapped(beside, "core")
    copies, key_grad, value_grad = second_sum(kept, got, 2 * copies_of)

    all_grads = lax.all_to_all(copies, ("dp", "yb"), 0, 0, tiled=True)
    blocks = weights_call(place, (late, *near_across, beside, beside_across), all_grads, depth)
    pieces = lax.all_to_all(blocks, group, 0, 0, tiled=True)
    spread = sum_rows(pieces, copies_of)
    weight = lax.all_to_all(spread, "dp", 0, 0, tiled=True).reshape(copies_of * rows, 2 * HEAD)
    query_grad = (dq_own + dq_far.astype(jnp.float32)).astype(jnp.bfloat16)[None]
    return (query_grad, key_grad[None], value_grad[None], weight[:, :HEAD], weight[:, HEAD:])


def solution(mesh):
    sizes = dict(mesh.shape)
    deep = sizes["ctx"] // 4
    fine = Mesh(
        mesh.devices.reshape(sizes["dp"], 2, 2, deep, 2, sizes["tp"] // 2),
        ("dp", "ya", "yb", "z", "yh", "core"),
    )
    context, model = ("ya", "yb", "z"), ("yh", "core")
    in_specs = (
        P("dp", context, model),
        P("dp", context, model),
        P("dp", context, model),
        P("dp", context, model),
        P("dp", context, model),
        P("dp", None),
        P(),
    )
    out_specs = (
        P("dp", context, model),
        P("dp", context, model),
        P("dp", context, model),
        P(context, model),
        P(context, model),
    )
    return jax.shard_map(shards, mesh=fine, in_specs=in_specs, out_specs=out_specs, check_vma=False)
```

```python
import jax
import jax.numpy as jnp
from jax import lax
from jax.experimental import pallas as pl
from jax.experimental.pallas import tpu as pltpu
from jax.sharding import Mesh, PartitionSpec as P

HEAD = 128
SPAN = 64
TILE = 256
SPANS_PER_TILE = TILE // SPAN
NEG = -1e30
SCALE = HEAD ** (-0.5)
LOG2E = 1.4426950408889634
VMEM_LIMIT = 16 * 1024 * 1024
SMALL_LIMIT = 8 * 1024 * 1024


def nt(left, right):
    return lax.dot_general(left, right, (((1,), (1,)), ((), ())), preferred_element_type=jnp.float32)


def tn(left, right):
    return lax.dot_general(left, right, (((0,), (0,)), ((), ())), preferred_element_type=jnp.float32)


def nn(left, right):
    return lax.dot_general(left, right, (((1,), (0,)), ((), ())), preferred_element_type=jnp.float32)


def load_operands(meta, own, other, kv, q_s, g_s, k_s, v_s, pos_s):
    rows = own.shape[1]
    for source, block in enumerate((own, other)):
        q_s[source * rows:(source + 1) * rows, :] = block[0]
        g_s[source * rows:(source + 1) * rows, :] = block[1]
    lane_rows = lax.broadcasted_iota(jnp.int32, (SPAN, 128), 0)

    def place(block, carry):
        for half in range(2):
            span = 2 * block + half
            start = pl.multiple_of(meta[0, span] * SPAN, SPAN)
            piece = kv[block, half * SPAN:(half + 1) * SPAN, :]
            k_s[pl.ds(start, SPAN), :] = piece[:, :HEAD]
            v_s[pl.ds(start, SPAN), :] = piece[:, HEAD:]
            pos_s[pl.ds(start, SPAN), :] = lane_rows + meta[1, span] * SPAN
        return carry

    lax.fori_loop(0, kv.shape[0], place, 0, unroll=True)


def masked_scores(k_tile, q_rows, pos_tile, q_pos, q_start):
    copies = q_rows.shape[0] // 128
    key_pos = jnp.concatenate([pos_tile] * copies, axis=1)
    mask = (key_pos - q_start).astype(jnp.uint32) <= (q_pos - q_start).astype(jnp.uint32)
    return jnp.where(mask, nt(k_tile, q_rows) * (SCALE * LOG2E), NEG)


def list_tiles(meta, items, together):
    def add(t, n, u):
        items[n] = u * 32 + t
        return n + 1

    count = jnp.int32(0)
    for u in range(4):
        count = lax.fori_loop(meta[2, u], meta[2, 4 + u], lambda t, n, u=u: add(t, n, u), count)
    for spare in range(together - 1):
        items[count + spare] = 4 * 32
    return lax.div(count + together - 1, together)


def tile_scores(item, qmeta, q_s, k_s, pos_s):
    u, t = lax.shift_right_logical(item, 5), item & 31
    here = pl.ds(pl.multiple_of(t * TILE, TILE), TILE)
    span = lax.rem(u, 4)
    rows = qmeta.shape[1]
    base = pl.ds(pl.multiple_of(span * rows, rows), rows)
    scores = masked_scores(
        k_s[here, :], q_s[base, :], pos_s[here, :], qmeta[pl.ds(2 * u, 1), :], qmeta[pl.ds(2 * u + 1, 1), :]
    )
    return span, base, here, t, scores


def stats_kernel(meta, qmeta, own, other, kv, out, q_s, g_s, k_s, v_s, pos_s, items):
    load_operands(meta, own, other, kv, q_s, g_s, k_s, v_s, pos_s)
    rows = qmeta.shape[1]
    out[0:4, :] = jnp.full((4, rows), NEG, jnp.float32)
    out[4:16, :] = jnp.zeros((12, rows), jnp.float32)
    groups = list_tiles(meta, items, 2)

    def group_step(group, carry):
        found = []
        for slot in range(2):
            span, base, here, t, scores = tile_scores(items[group * 2 + slot], qmeta, q_s, k_s, pos_s)
            top = jnp.max(scores, axis=0, keepdims=True)
            probs = jnp.exp2(scores - top)
            grad = nt(v_s[here, :], g_s[base, :])
            total = jnp.sum(probs, axis=0, keepdims=True)
            found.append((span, top, total, jnp.sum(probs * grad, axis=0, keepdims=True)))
        for span, top, total, weighted in found:
            before = out[pl.ds(span, 1), :]
            new_top = jnp.maximum(before, top)
            keep, scale = jnp.exp2(before - new_top), jnp.exp2(top - new_top)
            out[pl.ds(span, 1), :] = new_top
            out[pl.ds(4 + span, 1), :] = keep * out[pl.ds(4 + span, 1), :] + scale * total
            out[pl.ds(8 + span, 1), :] = keep * out[pl.ds(8 + span, 1), :] + scale * weighted
        return carry

    lax.fori_loop(0, groups, group_step, 0)


def grad_kernel(
    meta, qmeta, own, other, kv, stats, far, dq_own, dq_other, dkv,
    q_s, g_s, k_s, v_s, pos_s, items, dk_s, dv_s, dq_s, fin_s,
):
    load_operands(meta, own, other, kv, q_s, g_s, k_s, v_s, pos_s)
    rows = qmeta.shape[1]
    heads = rows // SPAN
    dk_s[...] = jnp.zeros_like(dk_s)
    dv_s[...] = jnp.zeros_like(dv_s)
    dq_s[...] = jnp.zeros_like(dq_s)
    for u in range(4):
        v = (u + 2) % 4
        top_a, top_b = stats[u:u + 1, :], far[v:v + 1, :]
        top = jnp.maximum(top_a, top_b)
        scale_a, scale_b = jnp.exp2(top_a - top), jnp.exp2(top_b - top)
        total = scale_a * stats[4 + u:5 + u, :] + scale_b * far[4 + v:5 + v, :]
        weighted = scale_a * stats[8 + u:9 + u, :] + scale_b * far[8 + v:9 + v, :]
        fin_s[u:u + 1, :] = top + jnp.log(total) * LOG2E
        fin_s[4 + u:5 + u, :] = weighted / total
    groups = list_tiles(meta, items, 2)

    def group_step(group, carry):
        found = []
        for slot in range(2):
            span, base, here, t, scores = tile_scores(items[group * 2 + slot], qmeta, q_s, k_s, pos_s)
            probs = jnp.exp2(scores - fin_s[pl.ds(span, 1), :])
            grad = nt(v_s[here, :], g_s[base, :])
            score_grad = (probs * (grad - fin_s[pl.ds(4 + span, 1), :])).astype(jnp.bfloat16)
            found.append((
                span, here, nn(probs.astype(jnp.bfloat16), g_s[base, :]), nn(score_grad, q_s[base, :]),
                tn(k_s[here, :], score_grad),
            ))
        for span, here, value_part, key_part, query_part in found:
            dv_s[here, :] += value_part
            dk_s[here, :] += key_part
            dq_s[span] += query_part
        return carry

    lax.fori_loop(0, groups, group_step, 0)
    for u in range(4):
        flat = (dq_s[u] * SCALE).T
        half = (u % 2) * SPAN
        for head in range(heads):
            piece = flat[head * SPAN:(head + 1) * SPAN, :]
            if u < 2:
                dq_own[half:half + SPAN, head * HEAD:(head + 1) * HEAD] = piece
            else:
                dq_other[half:half + SPAN, head * HEAD:(head + 1) * HEAD] = piece.astype(jnp.bfloat16)

    depth = dkv.shape[0] // 2

    def unplace(block, carry):
        for half in range(2):
            start = pl.multiple_of(meta[0, 2 * block + half] * SPAN, SPAN)
            here = pl.ds(start, SPAN)
            there = lax.rem(block, depth) * 2 + lax.div(block, depth)
            dkv[there, half * SPAN:(half + 1) * SPAN, :HEAD] = (dk_s[here, :] * SCALE).astype(jnp.bfloat16)
            dkv[there, half * SPAN:(half + 1) * SPAN, HEAD:] = dv_s[here, :].astype(jnp.bfloat16)
        return carry

    lax.fori_loop(0, dkv.shape[0], unplace, 0, unroll=True)


def operand_scratch(rows, keys):
    return [
        pltpu.VMEM((4 * rows, HEAD), jnp.bfloat16),
        pltpu.VMEM((4 * rows, HEAD), jnp.bfloat16),
        pltpu.VMEM((keys, HEAD), jnp.bfloat16),
        pltpu.VMEM((keys, HEAD), jnp.bfloat16),
        pltpu.VMEM((keys, 128), jnp.int32),
        pltpu.SMEM((4 * (keys // TILE) + 8,), jnp.int32),
    ]


def in_vmem(count):
    return [pl.BlockSpec(memory_space=pltpu.SMEM)] + [pl.BlockSpec(memory_space=pltpu.VMEM)] * count


def stats_call(meta, qmeta, own, other, kv):
    rows = qmeta.shape[1]
    keys = kv.shape[0] * kv.shape[1]
    return pl.pallas_call(
        stats_kernel,
        out_shape=jax.ShapeDtypeStruct((16, rows), jnp.float32),
        in_specs=in_vmem(4),
        out_specs=pl.BlockSpec(memory_space=pltpu.VMEM),
        scratch_shapes=operand_scratch(rows, keys),
        compiler_params=pltpu.CompilerParams(vmem_limit_bytes=VMEM_LIMIT),
        cost_estimate=pl.CostEstimate(flops=2 * 10**9, bytes_accessed=4 * 10**6, transcendentals=10**6),
        name="stats",
    )(meta, qmeta, own, other, kv)


def grad_call(meta, qmeta, own, other, kv, stats, far):
    rows = qmeta.shape[1]
    keys = kv.shape[0] * kv.shape[1]
    height, width = 2 * SPAN, rows // SPAN * HEAD
    return pl.pallas_call(
        grad_kernel,
        out_shape=(
            jax.ShapeDtypeStruct((height, width), jnp.float32),
            jax.ShapeDtypeStruct((height, width), jnp.bfloat16),
            jax.ShapeDtypeStruct(kv.shape, jnp.bfloat16),
        ),
        in_specs=in_vmem(6),
        out_specs=[pl.BlockSpec(memory_space=pltpu.VMEM)] * 3,
        scratch_shapes=operand_scratch(rows, keys) + [
            pltpu.VMEM((keys, HEAD), jnp.float32),
            pltpu.VMEM((keys, HEAD), jnp.float32),
            pltpu.VMEM((4, HEAD, rows), jnp.float32),
            pltpu.VMEM((8, rows), jnp.float32),
        ],
        compiler_params=pltpu.CompilerParams(vmem_limit_bytes=VMEM_LIMIT),
        cost_estimate=pl.CostEstimate(flops=5 * 10**9, bytes_accessed=6 * 10**6, transcendentals=10**6),
        name="grads",
    )(meta, qmeta, own, other, kv, stats, far)


def first_sum_kernel(place, parts, kept, sent):
    for where, out in ((place[3], kept), (1 - place[3], sent)):
        total = parts[where].astype(jnp.float32)
        for level in range(1, parts.shape[0] // 2):
            total += parts[2 * level + where].astype(jnp.float32)
        out[...] = total.astype(out.dtype)


def first_sum(place, parts):
    shape = parts.shape[1:]
    return pl.pallas_call(
        first_sum_kernel,
        out_shape=[jax.ShapeDtypeStruct(shape, jnp.float32), jax.ShapeDtypeStruct(shape, jnp.bfloat16)],
        in_specs=in_vmem(1),
        out_specs=[pl.BlockSpec(memory_space=pltpu.VMEM)] * 2,
        compiler_params=pltpu.CompilerParams(vmem_limit_bytes=SMALL_LIMIT),
        cost_estimate=pl.CostEstimate(flops=10**6, bytes_accessed=2 * 10**6, transcendentals=0),
        name="first_sum",
    )(place, parts)


def second_sum_kernel(kept, got, copies, key_out, value_out):
    rounded = (kept[...] + got[...].astype(jnp.float32)).astype(jnp.bfloat16)
    for copy in range(copies.shape[0]):
        copies[copy] = rounded
    key_out[...] = rounded[:, :HEAD]
    value_out[...] = rounded[:, HEAD:]


def second_sum(kept, got, count):
    height, width = kept.shape
    half = jax.ShapeDtypeStruct((height, HEAD), jnp.bfloat16)
    return pl.pallas_call(
        second_sum_kernel,
        out_shape=[jax.ShapeDtypeStruct((count, height, width), jnp.bfloat16), half, half],
        in_specs=[pl.BlockSpec(memory_space=pltpu.VMEM)] * 2,
        out_specs=[pl.BlockSpec(memory_space=pltpu.VMEM)] * 3,
        compiler_params=pltpu.CompilerParams(vmem_limit_bytes=SMALL_LIMIT),
        cost_estimate=pl.CostEstimate(flops=10**6, bytes_accessed=10**6, transcendentals=0),
        name="second_sum",
    )(kept, got)


def sum_rows_kernel(parts, copies):
    total = parts[0].astype(jnp.float32)
    for part in range(1, parts.shape[0]):
        total += parts[part].astype(jnp.float32)
    for copy in range(copies.shape[0]):
        copies[copy] = total


def sum_rows(parts, count):
    return pl.pallas_call(
        sum_rows_kernel,
        out_shape=jax.ShapeDtypeStruct((count,) + parts.shape[1:], jnp.float32),
        in_specs=[pl.BlockSpec(memory_space=pltpu.VMEM)],
        out_specs=pl.BlockSpec(memory_space=pltpu.VMEM),
        compiler_params=pltpu.CompilerParams(vmem_limit_bytes=SMALL_LIMIT),
        cost_estimate=pl.CostEstimate(flops=10**6, bytes_accessed=2 * 10**6, transcendentals=0),
        name="sum_rows",
    )(parts)


def weights_kernel(place, *refs):
    arrays, grads, out = refs[:-2], refs[-2], refs[-1]
    count = grads.shape[0] // 2
    rows = out.shape[1]
    slots = out.shape[0] // 2
    sources = [lax.rem(place[0] - back + count, count) * 2 for back in range(count)]
    here, there = place[2], 1 - place[2]
    right = jnp.concatenate([grads[s + here] for s in sources] + [grads[s + there] for s in sources], axis=0)
    slabs = [(ref, i) for ref in arrays for i in range(ref.shape[0])]
    each = len(slabs) // 2
    for high in range(2):
        blocks = [ref[i] for ref, i in slabs[high * each:(high + 1) * each]]
        result = nn(jnp.concatenate(blocks, axis=1), right).astype(jnp.bfloat16)
        block = lax.bitwise_xor(place[1], high)
        for slot in range(slots):
            out[block * slots + slot] = result[slot * rows:(slot + 1) * rows]


def weights_call(place, arrays, grads, slots):
    rows = arrays[0].shape[1] // slots
    return pl.pallas_call(
        weights_kernel,
        out_shape=jax.ShapeDtypeStruct((2 * slots, rows, grads.shape[2]), jnp.bfloat16),
        in_specs=in_vmem(1 + len(arrays)),
        out_specs=pl.BlockSpec(memory_space=pltpu.VMEM),
        compiler_params=pltpu.CompilerParams(vmem_limit_bytes=SMALL_LIMIT),
        cost_estimate=pl.CostEstimate(flops=10**9, bytes_accessed=4 * 10**6, transcendentals=0),
        name="weights",
    )(place, *arrays, grads)


def swapped(array, axis):
    return lax.ppermute(array, axis, [(0, 1), (1, 0)])


def tables(doc_lengths, span_order):
    count = span_order.shape[0]
    outer, inner = lax.axis_size("ya"), lax.axis_size("z")
    side = lax.axis_index("yb")
    boundary = jnp.cumsum(doc_lengths[0])
    order = span_order.reshape(outer, 2, inner)
    mine = jnp.where(side == 0, order[:, 0], order[:, 1]).reshape(-1)
    spans = jnp.stack([mine, 2 * count - 1 - mine], axis=1).reshape(-1)
    rank = jnp.sum((spans[None, :] < spans[:, None]).astype(jnp.int32), axis=1)
    ctx = lax.axis_index(("ya", "yb", "z"))
    ids = jnp.arange(count, dtype=jnp.int32)
    first = jnp.sum(jnp.where(ids == ctx, span_order, 0))
    partner = ctx + (1 - 2 * side) * inner
    second = jnp.sum(jnp.where(ids == partner, span_order, 0))
    q_spans = jnp.stack([first, 2 * count - 1 - first, second, 2 * count - 1 - second])

    def doc_start(positions):
        reached = boundary <= positions[..., None]
        return jnp.max(jnp.where(reached, boundary, 0), axis=-1)

    low = doc_start(q_spans * SPAN) // SPAN
    lower = jnp.sum((spans[None, :] < low[:, None]).astype(jnp.int32), axis=1) // SPANS_PER_TILE
    upper = jnp.sum((spans[None, :] <= q_spans[:, None]).astype(jnp.int32), axis=1)
    upper = (upper + SPANS_PER_TILE - 1) // SPANS_PER_TILE
    bounds = jnp.concatenate([lower, upper, jnp.zeros((spans.shape[0] - 8,), jnp.int32)])
    meta = jnp.stack([rank, spans, bounds])
    return meta, q_spans, doc_start


def shards(queries, keys, values, out_grad, normed_input, doc_lengths, span_order):
    height = queries.shape[1]
    heads = queries.shape[2] // HEAD
    group = ("ya", "z")
    group_size = lax.axis_size("ya") * lax.axis_size("z")
    depth = lax.axis_size("z")

    def laid(array):
        return array.reshape(2, SPAN, heads, HEAD).transpose(0, 2, 1, 3).reshape(heads * height, HEAD)

    own = jnp.stack([laid(queries[0]), laid(out_grad[0])])
    other = swapped(own, "yb")
    pair = jnp.concatenate([keys[0], values[0]], axis=1)
    kv = lax.all_to_all(
        jnp.broadcast_to(pair[None], (group_size,) + pair.shape), group, 0, 0, tiled=True
    )

    meta, q_spans, doc_start = tables(doc_lengths, span_order)
    q_pos = q_spans[:, None] * SPAN + jnp.arange(SPAN, dtype=jnp.int32)[None, :]
    q_start = doc_start(q_pos)
    qmeta = jnp.pad(jnp.stack([q_pos, q_start], axis=1).reshape(8, SPAN), ((0, 8), (0, 0)), constant_values=-1)
    qmeta = jnp.tile(qmeta, (1, heads))

    other, features = lax.optimization_barrier((other, normed_input))
    copies_of = lax.axis_size("dp")
    replica = lax.axis_index("dp")
    rows = normed_input.shape[2] // (depth * copies_of)
    slabs = features[0].reshape(height, depth, copies_of, rows).transpose(2, 1, 3, 0)
    slabs = slabs.reshape(copies_of, depth * rows, height)
    columns = []
    for by in range(copies_of):
        place = lax.rem(replica + by, copies_of)
        slab = lax.dynamic_index_in_dim(slabs, place, 0, keepdims=False)
        columns.append(
            lax.ppermute(
                slab,
                ("dp", "yb", "core"),
                [
                    (d * 4 + b * 2 + c, (d + by) % copies_of * 4 + c * 2 + b)
                    for d in range(copies_of) for b in range(2) for c in range(2)
                ],
            )
        )
    stats = stats_call(meta, qmeta, own, other, kv)
    stats, columns = lax.optimization_barrier((stats, columns))
    far = swapped(stats, "yb")
    far, near = lax.optimization_barrier((far, jnp.stack(columns)))
    dq_own, dq_other, dkv = grad_call(meta, qmeta, own, other, kv, stats, far)

    place = jnp.stack(
        [replica, lax.axis_index("yh"), lax.axis_index("core"), lax.axis_index("ya")]
    ).astype(jnp.int32)
    dkv, late = lax.optimization_barrier((dkv, near))
    beside = swapped(late, "yh")
    parts = lax.all_to_all(dkv, "z", 0, 0, tiled=True)
    halves = late[:copies_of // 2], late[copies_of // 2:]
    near_across = [swapped(part, "core") for part in halves]
    parts, near_across = lax.optimization_barrier((parts, near_across))
    kept, sent_grads = first_sum(place, parts)
    got = swapped(sent_grads, "ya")
    dq_far = swapped(dq_other, "yb")
    got, beside = lax.optimization_barrier((got, beside))
    beside_across = swapped(beside, "core")
    copies, key_grad, value_grad = second_sum(kept, got, 2 * copies_of)

    all_grads = lax.all_to_all(copies, ("dp", "yb"), 0, 0, tiled=True)
    blocks = weights_call(place, (late, *near_across, beside, beside_across), all_grads, depth)
    pieces = lax.all_to_all(blocks, group, 0, 0, tiled=True)
    spread = sum_rows(pieces, copies_of)
    weight = lax.all_to_all(spread, "dp", 0, 0, tiled=True).reshape(copies_of * rows, 2 * HEAD)
    query_grad = (dq_own + dq_far.astype(jnp.float32)).astype(jnp.bfloat16)[None]
    return (query_grad, key_grad[None], value_grad[None], weight[:, :HEAD], weight[:, HEAD:])


def solution(mesh):
    sizes = dict(mesh.shape)
    deep = sizes["ctx"] // 4
    fine = Mesh(
        mesh.devices.reshape(sizes["dp"], 2, 2, deep, 2, sizes["tp"] // 2),
        ("dp", "ya", "yb", "z", "yh", "core"),
    )
    context, model = ("ya", "yb", "z"), ("yh", "core")
    in_specs = (
        P("dp", context, model),
        P("dp", context, model),
        P("dp", context, model),
        P("dp", context, model),
        P("dp", context, model),
        P("dp", None),
        P(),
    )
    out_specs = (
        P("dp", context, model),
        P("dp", context, model),
        P("dp", context, model),
        P(context, model),
        P(context, model),
    )
    return jax.shard_map(shards, mesh=fine, in_specs=in_specs, out_specs=out_specs, check_vma=False)
```
